256 devices in a mesh: group: 128 (over z, y, x_hi, core), sp: 2 (over x_lo).
Axes of the slice: x: 4 (x_hi: 2, x_lo: 2; x = x_hi * 2 + x_lo), y: 4, z: 8, core: 2. Of those that a mesh axis runs over, the one named last changes fastest.
Arguments:
- query_frames: bfloat16 [1280, 64, 2560], P('group', 'sp'), may hold values from -6 to 6
- key_frames: bfloat16 [1280, 64, 2560], P('group', 'sp'), may hold values from -6 to 6
- value_frames: bfloat16 [1280, 64, 2560], P('group', 'sp'), may hold values from -6 to 6
- out_cotangent: bfloat16 [1024, 64, 2560], P('group', 'sp'), may hold values from -6 to 6
- frame_counts: int32 [128, 3], replicated, may hold values from 0 to 8, as said below
Outputs:
- attended: bfloat16 [1024, 64, 2560], P('group', 'sp')
- query_grad: bfloat16 [1280, 64, 2560], P('group', 'sp')
- key_grad: bfloat16 [1280, 64, 2560], P('group', 'sp')
- value_grad: bfloat16 [1280, 64, 2560], P('group', 'sp')
The draws below stay inside these ranges and needn't reach their ends.
Inputs may be any that keep to these rules, and one draw needn't show every extreme that they name: `frame_counts`: row g is (a, b, c) with a + b + c = 8 and a, c at most 1, groups counted modulo 128. Anchor group g holds, from slot 0 on, the c frames of row g-1, its own b frames, then the a frames of row g+1; its remaining slots are empty. In every draw some group holds all 10 slots, sending 1 frames to each neighbour.
All inputs are finite; a program needn't handle non-finite values.
Results may differ from the reference program's by a relative error of at most 0.0072.
Values may be sent and summed in bfloat16 or wider, within the bound.
A program may use at most 64 MiB of HBM per device.

```python
import math
import jax
import jax.numpy as jnp
from jax import lax

HEADS = 20
HDIM = 128
TPF = 64
F_DEST = 8
W = 2560
MAXF = 1
F_ORIG = 10
GROUPS = 128
ORIG_FRAMES = 1280
DEST_FRAMES = 1024


def draw_query_frames(key, part):
    key = jax.random.fold_in(key, 1)
    frames = jax.random.truncated_normal(key, -6.0, 6.0, (ORIG_FRAMES, TPF, W), jnp.float32)
    return frames.astype(jnp.bfloat16)


def draw_key_frames(key, part):
    key = jax.random.fold_in(key, 2)
    frames = jax.random.truncated_normal(key, -6.0, 6.0, (ORIG_FRAMES, TPF, W), jnp.float32)
    return frames.astype(jnp.bfloat16)


def draw_frame_counts(key, part):
    key = jax.random.fold_in(key, 5)
    capacity = MAXF
    take_low = jax.random.randint(jax.random.fold_in(key, 1), (GROUPS,), 0, capacity + 1)
    take_high = jax.random.randint(jax.random.fold_in(key, 2), (GROUPS,), 0, capacity + 1)
    chosen = jax.random.randint(jax.random.fold_in(key, 3), (), 0, GROUPS)
    group_ids = jnp.arange(GROUPS, dtype=jnp.int32)
    take_low = jnp.where(group_ids == chosen, 0, jnp.where(group_ids == (chosen + 1) % GROUPS, capacity, take_low))
    take_high = jnp.where(group_ids == chosen, 0, jnp.where(group_ids == (chosen - 1 + GROUPS) % GROUPS, capacity, take_high))
    native = F_DEST - take_low - take_high
    return jnp.stack([take_low, native, take_high], axis=1).astype(jnp.int32)


def level_of(own_key, extent, split, low, high):
    level, own = 1.0, jax.random.fold_in(own_key, 6)
    for dim, parts in split:
        draws = jnp.exp(jax.random.uniform(jax.random.fold_in(own, dim), (parts,), jnp.float32, low / len(split), high / len(split)))
        level = level * jnp.repeat(draws, extent[dim] // parts).reshape([-1 if axis == dim else 1 for axis in range(len(extent))])
    return level


def noise(key, dims, scale, limit, cuts=(), kind=jnp.bfloat16):
    drawn = scale * jax.random.normal(key, dims, jnp.float32)
    if cuts:
        drawn = drawn * level_of(key, dims, cuts, -0.22, 0.18)
    return jnp.clip(drawn, -limit, limit).astype(kind)


def setup_inputs(seed: int = 0) -> dict:
    keys = jax.random.split(jax.random.key(seed), 6)
    query_frames = draw_query_frames(jax.random.fold_in(keys[5], 71), 0)
    key_frames = draw_key_frames(jax.random.fold_in(keys[5], 71), 0)
    value_frames = noise(keys[2], (ORIG_FRAMES, TPF, W), 1.0, 6.0, ((0, 128), (1, 2)))
    out_cotangent = noise(keys[3], (DEST_FRAMES, TPF, W), 1.0, 6.0, ((0, 128), (1, 2)))
    frame_counts = draw_frame_counts(jax.random.fold_in(keys[5], 71), 0)
    return {"query_frames": query_frames, "key_frames": key_frames, "value_frames": value_frames, "out_cotangent": out_cotangent, "frame_counts": frame_counts}


def product(left, right):
    return jnp.dot(left.astype(jnp.float32), right.astype(jnp.float32), precision=lax.Precision.HIGHEST, preferred_element_type=jnp.float32)

def head_pass(queries, key_rows, value_rows, upstream, segment):
    scaling = 1.0 / math.sqrt(queries.shape[-1])
    same_clip = segment[:, None] == segment[None, :]
    logits = product(queries, key_rows.T) * scaling
    logits = jnp.where(same_clip, logits, -jnp.inf)
    row_max = lax.optimization_barrier(jnp.max(logits, axis=1, keepdims=True))
    powers = jnp.exp(logits - row_max)
    softmax = powers / lax.optimization_barrier(jnp.sum(powers, axis=1, keepdims=True))
    low_probs = softmax.astype(jnp.bfloat16)
    attended = product(low_probs, value_rows).astype(jnp.bfloat16)
    value_grad = product(low_probs.T, upstream).astype(jnp.bfloat16)
    prob_grad = product(upstream, value_rows.T)
    correction = lax.optimization_barrier(jnp.sum(softmax * prob_grad, axis=1, keepdims=True))
    logit_grad = (softmax * (prob_grad - correction)).astype(jnp.bfloat16)
    query_grad = (product(logit_grad, key_rows) * scaling).astype(jnp.bfloat16)
    key_grad = (product(logit_grad.T, queries) * scaling).astype(jnp.bfloat16)
    return (attended, query_grad, key_grad, value_grad)

def plan_sources(frame_counts):
    take_low = frame_counts[:, 0][:, None]
    native = frame_counts[:, 1][:, None]
    high_all = frame_counts[:, 2]
    group_ids = jnp.arange(GROUPS, dtype=jnp.int32)[:, None]
    slot_ids = jnp.arange(F_DEST, dtype=jnp.int32)[None, :]
    high_prev = jnp.roll(high_all, 1)[:, None]
    high_prev_two = jnp.roll(high_all, 2)[:, None]
    native_prev = jnp.roll(frame_counts[:, 1], 1)[:, None]
    from_lower = (group_ids - 1 + GROUPS) % GROUPS * F_ORIG + high_prev_two + native_prev + slot_ids
    from_self = group_ids * F_ORIG + high_prev + slot_ids - take_low
    from_upper = (group_ids + 1) % GROUPS * F_ORIG + slot_ids - take_low - native
    sources = jnp.where(slot_ids < take_low, from_lower, jnp.where(slot_ids < take_low + native, from_self, from_upper))
    labels = jnp.where(slot_ids < take_low, 0, jnp.where(slot_ids < take_low + native, 1, 2))
    return (sources.astype(jnp.int32), labels.astype(jnp.int32))

def reference(query_frames, key_frames, value_frames, out_cotangent, frame_counts):
    sources, labels = plan_sources(frame_counts)
    flat_sources = sources.reshape(-1)
    row_count = F_DEST * TPF

    def gathered(frames):
        return jnp.moveaxis(jnp.take(frames, flat_sources, axis=0).reshape(GROUPS, row_count, HEADS, HDIM), 2, 1)
    queries = gathered(query_frames)
    key_rows = gathered(key_frames)
    value_rows = gathered(value_frames)
    upstream = jnp.moveaxis(out_cotangent.reshape(GROUPS, row_count, HEADS, HDIM), 2, 1)
    segment_rows = jnp.repeat(labels, TPF, axis=1)

    def one_group(pieces):
        segment = pieces[4]

        def one_head(inner):
            return head_pass(inner[0], inner[1], inner[2], inner[3], segment)
        return lax.map(one_head, (pieces[0], pieces[1], pieces[2], pieces[3]))
    results = lax.map(one_group, (queries, key_rows, value_rows, upstream, segment_rows))

    def to_rows(result):
        return jnp.moveaxis(result, 1, 2).reshape(GROUPS * F_DEST, TPF, W)
    attended, query_grad, key_grad, value_grad = [to_rows(result) for result in results]

    def to_anchor(result):
        empty = jnp.zeros((GROUPS * F_ORIG, TPF, W), jnp.bfloat16)
        return empty.at[flat_sources].set(result)
    return (attended, to_anchor(query_grad), to_anchor(key_grad), to_anchor(value_grad))
```

```python
import functools
import math

import jax
import jax.numpy as jnp
from jax import lax
from jax.experimental import pallas as pl
from jax.experimental.pallas import tpu as pltpu
from jax.sharding import PartitionSpec as P

HDIM = 128
MESH = pl.DeviceIdType.MESH
AHEAD_SEND = 3
AHEAD_UP = 4
AHEAD_MOVE = 6
FIRST_HEADS = 4
ROW_BLOCKS = 4


def pick(cond, yes, no):
    return lax.select_n(cond, no, yes)


def kernel(
    groups,
    counts,
    q_hbm,
    k_hbm,
    v_hbm,
    do_hbm,
    o_hbm,
    dq_hbm,
    dk_hbm,
    dv_hbm,
    raw,
    own,
    peer,
    move_src,
    move_dst,
    grads,
    back_dst,
    o_stage,
    g_stage,
    cat,
    p_buf,
    ds_buf,
    bias,
    raw_sem,
    up_sem,
    move_send,
    move_recv,
    do_send,
    do_recv,
    qkv_send,
    qkv_recv,
    back_send,
    back_recv,
    o_sem,
    g_sem,
):
    heads = own.shape[0]
    dest = own.shape[2]
    orig = raw.shape[1]
    tokens = own.shape[3]
    half = dest * tokens
    rows = 2 * half
    scaling = 1.0 / math.sqrt(HDIM)
    exponent = scaling * math.log2(math.e)

    g = lax.axis_index("group")
    s = lax.axis_index("sp")
    core = g % 2
    upper = (g + 1) % groups
    lower = (g + groups - 1) % groups
    flip = 1 - 2 * s
    to_peer = {"group": g, "sp": 1 - s}
    to_upper = {"group": upper, "sp": s + core * flip}
    to_lower = {"group": lower, "sp": s + (1 - core) * flip}

    def cols(h):
        return pl.ds(pl.multiple_of(h * HDIM, HDIM), HDIM)

    def raw_load(array, part):
        split = FIRST_HEADS * HDIM
        span = pl.ds(0, split) if part == 0 else pl.ds(split, heads * HDIM - split)
        source = (q_hbm, k_hbm, v_hbm)[array]
        return pltpu.make_async_copy(
            source.at[:, :, span], raw.at[array, :, :, span], raw_sem.at[array, part]
        )

    def up_load(h):
        return pltpu.make_async_copy(do_hbm.at[:, :, cols(h)], own.at[h, 3], up_sem.at[h])

    def move(way, h):
        return pltpu.make_async_remote_copy(
            src_ref=move_src.at[way, h],
            dst_ref=move_dst.at[way, h],
            send_sem=move_send.at[way, h],
            recv_sem=move_recv.at[way, h],
            device_id=to_upper if way == 0 else to_lower,
            device_id_type=MESH,
        )

    def do_copy(h):
        return pltpu.make_async_remote_copy(
            src_ref=own.at[h, 3],
            dst_ref=peer.at[h, 3],
            send_sem=do_send.at[h],
            recv_sem=do_recv.at[h],
            device_id=to_peer,
            device_id_type=MESH,
        )

    def qkv_copy(h):
        return pltpu.make_async_remote_copy(
            src_ref=own.at[h, pl.ds(0, 3)],
            dst_ref=peer.at[h, pl.ds(0, 3)],
            send_sem=qkv_send.at[h],
            recv_sem=qkv_recv.at[h],
            device_id=to_peer,
            device_id_type=MESH,
        )

    def back(way, h):
        return pltpu.make_async_remote_copy(
            src_ref=grads.at[h, :, dest - 1 if way == 0 else 0],
            dst_ref=back_dst.at[way, h],
            send_sem=back_send.at[way, h],
            recv_sem=back_recv.at[way, h],
            device_id=to_upper if way == 0 else to_lower,
            device_id_type=MESH,
        )

    def o_store(h):
        return pltpu.make_async_copy(o_stage.at[h], o_hbm.at[:, :, cols(h)], o_sem.at[h])

    def g_store(array, h):
        target = (dq_hbm, dk_hbm, dv_hbm)[array]
        return pltpu.make_async_copy(
            g_stage.at[h, array], target.at[:, :, cols(h)], g_sem.at[array, h]
        )

    def each(low, high, action):
        def step(h, carry):
            action(h)
            return carry

        lax.fori_loop(low, high, step, 0)

    for array in range(3):
        raw_load(array, 0).start()
    each(0, heads, lambda h: up_load(h).start())
    for array in range(3):
        raw_load(array, 1).start()

    take_low = counts[g, 0]
    native = counts[g, 1]
    take_high = counts[g, 2]
    give_low = counts[lower, 2]
    give_high = counts[upper, 0]
    shift = give_low - take_low
    last_slot = give_low + native
    from_low = take_low == 1
    from_high = take_high == 1
    swap_low = jnp.logical_and(core == 0, from_low)
    swap_high = jnp.logical_and(core == 1, from_high)

    barrier = pltpu.get_barrier_semaphore()
    for device in (to_peer, to_upper, to_lower):
        pl.semaphore_signal(barrier, inc=1, device_id=device, device_id_type=MESH)
    pl.semaphore_wait(barrier, 3)

    def send_moves(h):
        for array in range(3):
            frame = raw[array, orig - 1, :, cols(h)]
            for slot in range(dest - 2, orig - 1):
                frame = pick(last_slot == slot, raw[array, slot, :, cols(h)], frame)
            move_src[0, h, array] = frame
            move_src[1, h, array] = raw[array, 0, :, cols(h)]
        move(0, h).start()
        move(1, h).start()

    def send_up(h):
        up_load(h).wait()
        do_copy(h).start()

    def send_qkv(h):
        move(0, h).wait_recv()
        move(1, h).wait_recv()
        for array in range(3):
            for slot in range(dest):
                frame = pick(
                    shift == 1, raw[array, slot + 1, :, cols(h)], raw[array, slot, :, cols(h)]
                )
                if slot > 0:
                    frame = pick(shift == -1, raw[array, slot - 1, :, cols(h)], frame)
                else:
                    frame = pick(from_low, move_dst[0, h, array], frame)
                if slot == dest - 1:
                    frame = pick(from_high, move_dst[1, h, array], frame)
                own[h, array, slot] = frame
        qkv_copy(h).start()

    for array in range(3):
        raw_load(array, 0).wait()
    each(0, FIRST_HEADS, send_moves)
    each(0, AHEAD_UP, send_up)
    for array in range(3):
        raw_load(array, 1).wait()
    each(FIRST_HEADS, AHEAD_MOVE, send_moves)
    each(0, AHEAD_SEND, send_qkv)

    def labels(dim):
        slot = (lax.broadcasted_iota(jnp.int32, (rows, rows), dim) // tokens) % dest
        low = jnp.where(slot == 0, take_low, 0)
        high = jnp.where(slot == dest - 1, take_high, 0)
        return high - low

    bias[...] = jnp.where(labels(0) == labels(1), 0.0, -jnp.inf)

    def rows_of(ref, h, array):
        return ref[h, array].reshape(half, HDIM)

    def dot(left, right, dims):
        return lax.dot_general(
            left, right, (dims, ((), ())), preferred_element_type=jnp.float32
        )

    def compute(h):
        for array in range(3):
            cat[array, :half] = rows_of(own, h, array)
            cat[array, half:] = rows_of(peer, h, array)
        cat[3, :half] = rows_of(own, h, 3)
        cat[3, half:] = rows_of(peer, h, 3)
        for swap, slot in ((swap_low, 0), (swap_high, dest - 1)):
            mine, other = own[h, 3, slot], peer[h, 3, slot]
            cat[3, pl.ds(slot * tokens, tokens)] = pick(swap, other, mine)
            cat[3, pl.ds(half + slot * tokens, tokens)] = pick(swap, mine, other)
        size = rows // ROW_BLOCKS
        for block in range(ROW_BLOCKS):
            span = pl.ds(block * size, size)
            logits = dot(cat[0, span], cat[1], ((1,), (1,))) * exponent + bias[span]
            powers = jnp.exp2(logits - jnp.max(logits, axis=1, keepdims=True))
            softmax = powers * (1.0 / jnp.sum(powers, axis=1, keepdims=True))
            p_buf[span] = softmax.astype(jnp.bfloat16)
            prob_grad = dot(cat[3, span], cat[2], ((1,), (1,)))
            correction = jnp.sum(softmax * prob_grad, axis=1, keepdims=True)
            ds_buf[span] = (softmax * (prob_grad - correction)).astype(jnp.bfloat16)
        edge = half - tokens
        probs = jnp.concatenate(
            [
                pick(swap_low, p_buf[half : half + tokens], p_buf[:tokens]),
                p_buf[tokens:edge],
                pick(swap_high, p_buf[half + edge :], p_buf[edge:half]),
            ],
            axis=0,
        )
        shape = (dest, tokens, HDIM)
        attended = dot(probs, cat[2], ((1,), (0,)))
        o_stage[h] = attended.astype(jnp.bfloat16).reshape(shape)
        query_grad = dot(ds_buf[:half], cat[1], ((1,), (0,))) * scaling
        grads[h, 0] = query_grad.astype(jnp.bfloat16).reshape(shape)
        key_grad = dot(ds_buf[:, :half], cat[0], ((0,), (0,))) * scaling
        grads[h, 1] = key_grad.astype(jnp.bfloat16).reshape(shape)
        value_grad = dot(p_buf[:, :half], cat[3], ((0,), (0,)))
        grads[h, 2] = value_grad.astype(jnp.bfloat16).reshape(shape)

    def assemble(h):
        back(0, h).wait_recv()
        back(1, h).wait_recv()
        zero = jnp.zeros((tokens, HDIM), jnp.bfloat16)
        for array in range(3):
            for slot in range(orig):

                def source(index):
                    return grads[h, array, index] if 0 <= index < dest else zero

                frame = pick(shift == 1, source(slot - 1), source(slot))
                frame = pick(shift == -1, source(slot + 1), frame)
                inside = jnp.logical_and(slot >= give_low, slot < last_slot)
                frame = pick(inside, frame, zero)
                if slot == 0:
                    frame = pick(give_low == 1, back_dst[0, h, array], frame)
                if slot >= dest - 2:
                    top = jnp.logical_and(last_slot == slot, give_high == 1)
                    frame = pick(top, back_dst[1, h, array], frame)
                g_stage[h, array, slot] = frame
            g_store(array, h).start()

    def step(h):
        @pl.when(h + AHEAD_SEND < heads)
        def _():
            send_qkv(h + AHEAD_SEND)

        @pl.when(h + AHEAD_UP < heads)
        def _():
            send_up(h + AHEAD_UP)

        @pl.when(h + AHEAD_MOVE < heads)
        def _():
            send_moves(h + AHEAD_MOVE)

        do_copy(h).wait_recv()
        qkv_copy(h).wait_recv()
        compute(h)
        back(0, h).start()
        back(1, h).start()
        o_store(h).start()

        @pl.when(h > 0)
        def _():
            assemble(h - 1)

    each(0, heads, step)
    assemble(heads - 1)

    def finish(h):
        do_copy(h).wait_send()
        qkv_copy(h).wait_send()
        for way in range(2):
            move(way, h).wait_send()
            back(way, h).wait_send()
        o_store(h).wait()
        for array in range(3):
            g_store(array, h).wait()

    each(0, heads, finish)


def body(query_frames, key_frames, value_frames, out_cotangent, frame_counts):
    groups = lax.axis_size("group")
    orig, tokens, width = query_frames.shape
    dest = out_cotangent.shape[0]
    heads = width // HDIM
    rows = 2 * dest * tokens
    bf16 = jnp.bfloat16
    anywhere = pl.BlockSpec(memory_space=pl.ANY)
    anchor = jax.ShapeDtypeStruct((orig, tokens, width), bf16)
    attending = jax.ShapeDtypeStruct((dest, tokens, width), bf16)
    dma = pltpu.SemaphoreType.DMA
    return pl.pallas_call(
        functools.partial(kernel, groups),
        out_shape=(attending, anchor, anchor, anchor),
        in_specs=[pl.BlockSpec(memory_space=pltpu.SMEM)] + [anywhere] * 4,
        out_specs=(anywhere,) * 4,
        scratch_shapes=[
            pltpu.VMEM((3, orig, tokens, width), bf16),
            pltpu.VMEM((heads, 4, dest, tokens, HDIM), bf16),
            pltpu.VMEM((heads, 4, dest, tokens, HDIM), bf16),
            pltpu.VMEM((2, heads, 3, tokens, HDIM), bf16),
            pltpu.VMEM((2, heads, 3, tokens, HDIM), bf16),
            pltpu.VMEM((heads, 3, dest, tokens, HDIM), bf16),
            pltpu.VMEM((2, heads, 3, tokens, HDIM), bf16),
            pltpu.VMEM((heads, dest, tokens, HDIM), bf16),
            pltpu.VMEM((heads, 3, orig, tokens, HDIM), bf16),
            pltpu.VMEM((4, rows, HDIM), bf16),
            pltpu.VMEM((rows, rows), bf16),
            pltpu.VMEM((rows, rows), bf16),
            pltpu.VMEM((rows, rows), jnp.float32),
            dma((3, 2)),
            dma((heads,)),
            dma((2, heads)),
            dma((2, heads)),
            dma((heads,)),
            dma((heads,)),
            dma((heads,)),
            dma((heads,)),
            dma((2, heads)),
            dma((2, heads)),
            dma((heads,)),
            dma((3, heads)),
        ],
        compiler_params=pltpu.CompilerParams(
            collective_id=0, has_side_effects=True, vmem_limit_bytes=52 << 20
        ),
    )(frame_counts, query_frames, key_frames, value_frames, out_cotangent)


def solution(mesh):
    spread = P("group", "sp", None)
    return jax.shard_map(
        body,
        mesh=mesh,
        in_specs=(spread, spread, spread, spread, P()),
        out_specs=(spread,) * 4,
        check_vma=False,
    )
```

```python
import functools
import math

import jax
import jax.numpy as jnp
from jax import lax
from jax.experimental import pallas as pl
from jax.experimental.pallas import tpu as pltpu
from jax.sharding import PartitionSpec as P

HDIM = 128
MESH = pl.DeviceIdType.MESH
CHUNKS = 5
AHEAD = 4
EDGE_UNROLL = 4
GATHER_FROM = 14
ROW_BLOCKS = 4


def pick(cond, yes, no):
    return lax.select_n(cond, no, yes)


def kernel(
    groups,
    counts,
    q_hbm,
    k_hbm,
    v_hbm,
    do_hbm,
    o_out,
    dq_out,
    dk_out,
    dv_out,
    raw,
    own_do,
    peer_do,
    own_edge,
    peer_edge,
    own_mid,
    peer_mid,
    move_src,
    move_dst,
    back_src,
    back_dst,
    grads,
    cat,
    p_buf,
    ds_buf,
    bias,
    raw_sem,
    up_sem,
    move_send,
    move_recv,
    do_send,
    do_recv,
    edge_send,
    edge_recv,
    mid_send,
    mid_recv,
    back_send,
    back_recv,
):
    heads = own_mid.shape[0]
    dest, tokens, _ = own_do.shape
    orig = raw.shape[1]
    inner = dest - 2
    half = dest * tokens
    rows = 2 * half
    scaling = 1.0 / math.sqrt(HDIM)
    exponent = scaling * math.log2(math.e)
    edge_slots = (0, dest - 1)
    group_heads = heads // CHUNKS

    g = lax.axis_index("group")
    s = lax.axis_index("sp")
    core = g % 2
    upper = (g + 1) % groups
    lower = (g + groups - 1) % groups
    flip = 1 - 2 * s
    to_peer = {"group": g, "sp": 1 - s}
    to_upper = {"group": upper, "sp": s + core * flip}
    to_lower = {"group": lower, "sp": s + (1 - core) * flip}

    def cols(h):
        return pl.ds(pl.multiple_of(h * HDIM, HDIM), HDIM)

    def raw_load(array):
        source = (q_hbm, k_hbm, v_hbm)[array]
        return pltpu.make_async_copy(source, raw.at[array], raw_sem.at[array])

    up_load = pltpu.make_async_copy(do_hbm, own_do, up_sem)

    def remote(src, dst, send, recv, device):
        return pltpu.make_async_remote_copy(
            src_ref=src,
            dst_ref=dst,
            send_sem=send,
            recv_sem=recv,
            device_id=device,
            device_id_type=MESH,
        )

    def move(way):
        source = move_src if way == 0 else raw.at[:, 0]
        return remote(
            source,
            move_dst.at[way],
            move_send.at[way],
            move_recv.at[way],
            to_upper if way == 0 else to_lower,
        )

    def do_copy(chunk):
        span = pl.ds(chunk * group_heads * HDIM, group_heads * HDIM)
        return remote(
            do_hbm.at[:, :, span],
            peer_do.at[:, :, span],
            do_send.at[chunk],
            do_recv.at[chunk],
            to_peer,
        )

    def edge_copy(chunk):
        span = pl.ds(chunk * group_heads, group_heads)
        return remote(
            own_edge.at[span],
            peer_edge.at[span],
            edge_send.at[chunk],
            edge_recv.at[chunk],
            to_peer,
        )

    def mid_copy(h):
        return remote(own_mid.at[h], peer_mid.at[h], mid_send.at[h], mid_recv.at[h], to_peer)

    def back(way):
        return remote(
            back_src.at[way],
            back_dst.at[way],
            back_send.at[way],
            back_recv.at[way],
            to_upper if way == 0 else to_lower,
        )

    def each(low, high, action):
        def step(h, carry):
            action(h)
            return carry

        lax.fori_loop(low, high, step, 0)

    for array in range(3):
        raw_load(array).start()
    up_load.start()

    take_low = counts[0, g]
    native = counts[1, g]
    take_high = counts[2, g]
    give_low = counts[2, lower]
    give_high = counts[0, upper]
    shift = give_low - take_low
    last_slot = give_low + native
    from_low = take_low == 1
    from_high = take_high == 1
    swap_low = jnp.logical_and(core == 0, from_low)
    swap_high = jnp.logical_and(core == 1, from_high)

    barrier = pltpu.get_barrier_semaphore()
    for device in (to_peer, to_upper, to_lower):
        pl.semaphore_signal(barrier, inc=1, device_id=device, device_id_type=MESH)
    pl.semaphore_wait(barrier, 3)

    for chunk in range(CHUNKS):
        do_copy(chunk).start()

    for array in range(3):
        raw_load(array).wait()

    def stage_move(h):
        for array in range(3):
            frame = raw[array, orig - 1, :, cols(h)]
            for slot in range(inner, orig - 1):
                frame = pick(last_slot == slot, raw[array, slot, :, cols(h)], frame)
            move_src[array, :, cols(h)] = frame

    move(1).start()
    each(0, heads, stage_move)
    move(0).start()

    def native_frame(h, array, slot):
        here = raw[array, slot, :, cols(h)]
        frame = pick(shift == 1, raw[array, slot + 1, :, cols(h)], here)
        if slot > 0:
            frame = pick(shift == -1, raw[array, slot - 1, :, cols(h)], frame)
        return frame

    def stage_mid(h):
        for array in range(3):
            for slot in range(inner):
                own_mid[h, array, slot] = native_frame(h, array, slot + 1)

    each(0, heads, stage_mid)

    def labels(dim):
        slot = (lax.broadcasted_iota(jnp.int32, (rows, rows), dim) // tokens) % dest
        low = jnp.where(slot == 0, take_low, 0)
        high = jnp.where(slot == dest - 1, take_high, 0)
        return high - low

    bias[...] = jnp.where(labels(0) == labels(1), 0.0, -jnp.inf)

    move(0).wait_recv()
    move(1).wait_recv()

    def stage_edge(h):
        for array in range(3):
            for way, (slot, moved) in enumerate(((0, from_low), (dest - 1, from_high))):
                frame = native_frame(h, array, slot)
                own_edge[h, array, way] = pick(moved, move_dst[way, array, :, cols(h)], frame)

    for chunk in range(CHUNKS):
        each(chunk * group_heads, (chunk + 1) * group_heads, stage_edge)
        edge_copy(chunk).start()

    def dot(left, right, dims):
        return lax.dot_general(
            left, right, (dims, ((), ())), preferred_element_type=jnp.float32
        )

    def attend(queries, keys, values, upstream, mask):
        logits = dot(queries, keys, ((1,), (1,))) * exponent + mask
        powers = jnp.exp2(logits - jnp.max(logits, axis=1, keepdims=True))
        softmax = powers * (1.0 / jnp.sum(powers, axis=1, keepdims=True))
        prob_grad = dot(upstream, values, ((1,), (1,)))
        correction = jnp.sum(softmax * prob_grad, axis=1, keepdims=True)
        logit_grad = softmax * (prob_grad - correction)
        return softmax.astype(jnp.bfloat16), logit_grad.astype(jnp.bfloat16)

    def edge_up(h, way):
        slot, swap = ((0, swap_low), (dest - 1, swap_high))[way]
        mine, other = own_do[slot, :, cols(h)], peer_do[slot, :, cols(h)]
        return pick(swap, other, mine), pick(swap, mine, other)

    edge_row = lax.broadcasted_iota(jnp.int32, (4 * tokens, 4 * tokens), 0) // tokens % 2
    edge_col = lax.broadcasted_iota(jnp.int32, (4 * tokens, 4 * tokens), 1) // tokens % 2
    edge_mask = jnp.where(edge_row == edge_col, 0.0, -jnp.inf)

    def edge_compute(h):
        def joined(array):
            both = [ref[h, array].reshape(2 * tokens, HDIM) for ref in (own_edge, peer_edge)]
            return jnp.concatenate(both, axis=0)

        queries, keys, values = joined(0), joined(1), joined(2)
        (low, far_low), (high, far_high) = edge_up(h, 0), edge_up(h, 1)
        upstream = jnp.concatenate([low, high, far_low, far_high], axis=0)
        probs, logit_grad = attend(queries, keys, values, upstream, edge_mask)
        mine = 2 * tokens
        query_grad = dot(logit_grad[:mine], keys, ((1,), (0,))) * scaling
        key_grad = dot(logit_grad[:, :mine], queries, ((0,), (0,))) * scaling
        value_grad = dot(probs[:, :mine], upstream, ((0,), (0,)))
        for array, grad in enumerate((query_grad, key_grad, value_grad)):
            grad = grad.astype(jnp.bfloat16)
            back_src[1, h, array] = grad[:tokens]
            back_src[0, h, array] = grad[tokens:]

    def compute(h):
        edge = half - tokens
        for array in range(3):
            for base, edges, mids in ((0, own_edge, own_mid), (half, peer_edge, peer_mid)):
                cat[array, pl.ds(base, tokens)] = edges[h, array, 0]
                cat[array, pl.ds(base + tokens, edge - tokens)] = mids[h, array].reshape(
                    edge - tokens, HDIM
                )
                cat[array, pl.ds(base + edge, tokens)] = edges[h, array, 1]
        for slot in range(1, dest - 1):
            cat[3, pl.ds(slot * tokens, tokens)] = own_do[slot, :, cols(h)]
            cat[3, pl.ds(half + slot * tokens, tokens)] = peer_do[slot, :, cols(h)]
        for way, slot in enumerate(edge_slots):
            mine, other = edge_up(h, way)
            cat[3, pl.ds(slot * tokens, tokens)] = mine
            cat[3, pl.ds(half + slot * tokens, tokens)] = other
        size = rows // ROW_BLOCKS
        for block in range(ROW_BLOCKS):
            span = pl.ds(block * size, size)
            p_buf[span], ds_buf[span] = attend(
                cat[0, span], cat[1], cat[2], cat[3, span], bias[span]
            )
        probs = jnp.concatenate(
            [
                pick(swap_low, p_buf[half : half + tokens], p_buf[:tokens]),
                p_buf[tokens:edge],
                pick(swap_high, p_buf[half + edge :], p_buf[edge:half]),
            ],
            axis=0,
        )
        shape = (dest, tokens, HDIM)
        attended = dot(probs, cat[2], ((1,), (0,)))
        o_out[:, :, cols(h)] = attended.astype(jnp.bfloat16).reshape(shape)
        query_grad = dot(ds_buf[:half], cat[1], ((1,), (0,))) * scaling
        grads[h, 0] = query_grad.astype(jnp.bfloat16).reshape(shape)
        key_grad = dot(ds_buf[:, :half], cat[0], ((0,), (0,))) * scaling
        grads[h, 1] = key_grad.astype(jnp.bfloat16).reshape(shape)
        value_grad = dot(p_buf[:, :half], cat[3], ((0,), (0,)))
        grads[h, 2] = value_grad.astype(jnp.bfloat16).reshape(shape)

    def assemble(h):
        zero = jnp.zeros((tokens, HDIM), jnp.bfloat16)
        for array in range(3):
            for slot in range(orig):

                def source(index):
                    return grads[h, array, index] if 0 <= index < dest else zero

                frame = pick(shift == 1, source(slot - 1), source(slot))
                frame = pick(shift == -1, source(slot + 1), frame)
                inside = jnp.logical_and(slot >= give_low, slot < last_slot)
                frame = pick(inside, frame, zero)
                if slot == 0:
                    frame = pick(give_low == 1, back_dst[0, h, array], frame)
                if slot >= inner:
                    top = jnp.logical_and(last_slot == slot, give_high == 1)
                    frame = pick(top, back_dst[1, h, array], frame)
                (dq_out, dk_out, dv_out)[array][slot, :, cols(h)] = frame

    up_load.wait()
    for chunk in range(CHUNKS):
        do_copy(chunk).wait_send()
    each(0, AHEAD, lambda h: mid_copy(h).start())
    for chunk in range(CHUNKS):
        do_copy(chunk).wait_recv()
    for chunk in range(CHUNKS):
        edge_copy(chunk).wait_recv()

        def edge_step(step, carry):
            for part in range(EDGE_UNROLL):
                edge_compute(step * EDGE_UNROLL + part)
            return carry

        count = group_heads // EDGE_UNROLL
        lax.fori_loop(chunk * count, (chunk + 1) * count, edge_step, 0)
    back(0).start()
    back(1).start()

    def main_step(h):
        @pl.when(h + AHEAD < heads)
        def _():
            mid_copy(h + AHEAD).start()

        mid_copy(h).wait_recv()
        compute(h)

        @pl.when(h == GATHER_FROM)
        def _():
            back(0).wait_recv()
            back(1).wait_recv()
            each(0, GATHER_FROM, assemble)

        @pl.when(h >= GATHER_FROM)
        def _():
            assemble(h)

    each(0, heads, main_step)

    for chunk in range(CHUNKS):
        edge_copy(chunk).wait_send()
    for way in range(2):
        move(way).wait_send()
        back(way).wait_send()
    each(0, heads, lambda h: mid_copy(h).wait_send())


def store_kernel(*refs):
    count = (len(refs) - 1) // 2
    sems = refs[-1]
    copies = [
        pltpu.make_async_copy(refs[i], refs[count + i], sems.at[i]) for i in range(count)
    ]
    for copy in copies:
        copy.start()
    for copy in copies:
        copy.wait()


def body(query_frames, key_frames, value_frames, out_cotangent, frame_counts):
    groups = lax.axis_size("group")
    orig, tokens, width = query_frames.shape
    dest = out_cotangent.shape[0]
    heads = width // HDIM
    rows = 2 * dest * tokens
    bf16 = jnp.bfloat16
    anywhere = pl.BlockSpec(memory_space=pl.ANY)
    in_vmem = pl.BlockSpec(memory_space=pltpu.VMEM)
    anchor = (orig, tokens, width)
    attending = (dest, tokens, width)
    dma = pltpu.SemaphoreType.DMA
    shapes = (attending, anchor, anchor, anchor)
    results = pl.pallas_call(
        functools.partial(kernel, groups),
        out_shape=tuple(pltpu.VMEM(shape, bf16) for shape in shapes),
        in_specs=[pl.BlockSpec(memory_space=pltpu.SMEM)] + [anywhere] * 4,
        out_specs=(in_vmem,) * 4,
        scratch_shapes=[
            pltpu.VMEM((3,) + anchor, bf16),
            pltpu.VMEM(attending, bf16),
            pltpu.VMEM(attending, bf16),
            pltpu.VMEM((heads, 3, 2, tokens, HDIM), bf16),
            pltpu.VMEM((heads, 3, 2, tokens, HDIM), bf16),
            pltpu.VMEM((heads, 3, dest - 2, tokens, HDIM), bf16),
            pltpu.VMEM((heads, 3, dest - 2, tokens, HDIM), bf16),
            pltpu.VMEM((3, tokens, width), bf16),
            pltpu.VMEM((2, 3, tokens, width), bf16),
            pltpu.VMEM((2, heads, 3, tokens, HDIM), bf16),
            pltpu.VMEM((2, heads, 3, tokens, HDIM), bf16),
            pltpu.VMEM((heads, 3, dest, tokens, HDIM), bf16),
            pltpu.VMEM((4, rows, HDIM), bf16),
            pltpu.VMEM((rows, rows), bf16),
            pltpu.VMEM((rows, rows), bf16),
            pltpu.VMEM((rows, rows), jnp.float32),
            dma((3,)),
            dma,
            dma((2,)),
            dma((2,)),
            dma((CHUNKS,)),
            dma((CHUNKS,)),
            dma((CHUNKS,)),
            dma((CHUNKS,)),
            dma((heads,)),
            dma((heads,)),
            dma((2,)),
            dma((2,)),
        ],
        compiler_params=pltpu.CompilerParams(
            collective_id=0, has_side_effects=True, vmem_limit_bytes=56 << 20
        ),
    )(frame_counts.T, query_frames, key_frames, value_frames, out_cotangent)
    return pl.pallas_call(
        store_kernel,
        out_shape=tuple(jax.ShapeDtypeStruct(shape, bf16) for shape in shapes),
        in_specs=[in_vmem] * 4,
        out_specs=(anywhere,) * 4,
        scratch_shapes=[dma((4,))],
        compiler_params=pltpu.CompilerParams(vmem_limit_bytes=8 << 20),
    )(*results)


def solution(mesh):
    spread = P("group", "sp", None)
    return jax.shard_map(
        body,
        mesh=mesh,
        in_specs=(spread, spread, spread, spread, P()),
        out_specs=(spread,) * 4,
        check_vma=False,
    )
```

```python
import functools
import math

import jax
import jax.numpy as jnp
from jax import lax
from jax.experimental import pallas as pl
from jax.experimental.pallas import tpu as pltpu
from jax.sharding import PartitionSpec as P

HDIM = 128
SCALING = 1.0 / math.sqrt(HDIM)
EXPONENT = SCALING * math.log2(math.e)
MESH = pl.DeviceIdType.MESH
CHUNKS = 5
AHEAD = 4
EDGE_UNROLL = 4
GATHER_FROM = 14
ROW_BLOCKS = 4


def pick(cond, yes, no):
    return lax.select_n(cond, no, yes)


def dot(left, right, dims):
    return lax.dot_general(left, right, (dims, ((), ())), preferred_element_type=jnp.float32)


def attend(queries, keys, values, upstream, mask):
    logits = dot(queries, keys, ((1,), (1,))) * EXPONENT + mask
    powers = jnp.exp2(logits - jnp.max(logits, axis=1, keepdims=True))
    softmax = powers * (1.0 / jnp.sum(powers, axis=1, keepdims=True))
    prob_grad = dot(upstream, values, ((1,), (1,)))
    correction = jnp.sum(softmax * prob_grad, axis=1, keepdims=True)
    logit_grad = softmax * (prob_grad - correction)
    return softmax.astype(jnp.bfloat16), logit_grad.astype(jnp.bfloat16)


def attend_head(plan, shape, cat, bias, p_buf, ds_buf):
    tokens = shape[1]
    rows = cat.shape[1]
    half = rows // 2
    edge = half - tokens
    size = rows // ROW_BLOCKS
    for block in range(ROW_BLOCKS):
        span = pl.ds(block * size, size)
        p_buf[span], ds_buf[span] = attend(cat[0, span], cat[1], cat[2], cat[3, span], bias[span])
    probs = jnp.concatenate(
        [
            pick(plan.swap_low, p_buf[half : half + tokens], p_buf[:tokens]),
            p_buf[tokens:edge],
            pick(plan.swap_high, p_buf[half + edge :], p_buf[edge:half]),
        ],
        axis=0,
    )
    attended = dot(probs, cat[2], ((1,), (0,)))
    query_grad = dot(ds_buf[:half], cat[1], ((1,), (0,))) * SCALING
    key_grad = dot(ds_buf[:, :half], cat[0], ((0,), (0,))) * SCALING
    value_grad = dot(p_buf[:, :half], cat[3], ((0,), (0,)))
    results = (attended, query_grad, key_grad, value_grad)
    return [result.astype(jnp.bfloat16).reshape(shape) for result in results]


class Plan:
    def __init__(self, counts, groups):
        g = lax.axis_index("group")
        core = g % 2
        upper = (g + 1) % groups
        lower = (g + groups - 1) % groups
        self.take_low = counts[0, g]
        self.take_high = counts[2, g]
        self.give_low = counts[2, lower]
        self.give_high = counts[0, upper]
        self.shift = self.give_low - self.take_low
        self.last_slot = self.give_low + counts[1, g]
        self.from_low = self.take_low == 1
        self.from_high = self.take_high == 1
        self.swap_low = jnp.logical_and(core == 0, self.from_low)
        self.swap_high = jnp.logical_and(core == 1, self.from_high)


def anchor_frame(plan, slot, dest, grad, low_back, high_back):
    zero = jnp.zeros_like(low_back)

    def source(index):
        return grad(index) if 0 <= index < dest else zero

    frame = pick(plan.shift == 1, source(slot - 1), source(slot))
    frame = pick(plan.shift == -1, source(slot + 1), frame)
    inside = jnp.logical_and(slot >= plan.give_low, slot < plan.last_slot)
    frame = pick(inside, frame, zero)
    if slot == 0:
        frame = pick(plan.give_low == 1, low_back, frame)
    if slot >= dest - 2:
        top = jnp.logical_and(plan.last_slot == slot, plan.give_high == 1)
        frame = pick(top, high_back, frame)
    return frame


def kernel(
    groups,
    counts_hbm,
    q_hbm,
    k_hbm,
    v_hbm,
    do_hbm,
    o_out,
    dq_out,
    dk_out,
    dv_out,
    cat,
    bias,
    last_back,
    counts,
    raw,
    own_do,
    peer_do,
    own_edge,
    peer_edge,
    own_mid,
    peer_mid,
    move_src,
    move_dst,
    back_src,
    back_dst,
    grads,
    p_buf,
    ds_buf,
    ready,
    counts_sem,
    raw_sem,
    up_sem,
    move_send,
    move_recv,
    do_send,
    do_recv,
    edge_send,
    edge_recv,
    mid_send,
    mid_recv,
    back_send,
    back_recv,
):
    heads = own_mid.shape[0]
    dest, tokens, _ = own_do.shape
    orig = raw.shape[1]
    inner = dest - 2
    half = dest * tokens
    rows = 2 * half
    edge_slots = (0, dest - 1)
    group_heads = heads // CHUNKS

    g = lax.axis_index("group")
    s = lax.axis_index("sp")
    core = g % 2
    upper = (g + 1) % groups
    lower = (g + groups - 1) % groups
    flip = 1 - 2 * s
    to_peer = {"group": g, "sp": 1 - s}
    to_upper = {"group": upper, "sp": s + core * flip}
    to_lower = {"group": lower, "sp": s + (1 - core) * flip}

    def cols(h):
        return pl.ds(pl.multiple_of(h * HDIM, HDIM), HDIM)

    def raw_load(array):
        source = (q_hbm, k_hbm, v_hbm)[array]
        return pltpu.make_async_copy(source, raw.at[array], raw_sem.at[array])

    up_load = pltpu.make_async_copy(do_hbm, own_do, up_sem)

    def remote(src, dst, send, recv, device):
        return pltpu.make_async_remote_copy(
            src_ref=src,
            dst_ref=dst,
            send_sem=send,
            recv_sem=recv,
            device_id=device,
            device_id_type=MESH,
        )

    def move(way):
        source = move_src if way == 0 else raw.at[:, 0]
        return remote(
            source,
            move_dst.at[way],
            move_send.at[way],
            move_recv.at[way],
            to_upper if way == 0 else to_lower,
        )

    def do_copy(chunk):
        span = pl.ds(chunk * group_heads * HDIM, group_heads * HDIM)
        return remote(
            do_hbm.at[:, :, span],
            peer_do.at[:, :, span],
            do_send.at[chunk],
            do_recv.at[chunk],
            to_peer,
        )

    def edge_copy(chunk):
        span = pl.ds(chunk * group_heads, group_heads)
        return remote(
            own_edge.at[span],
            peer_edge.at[span],
            edge_send.at[chunk],
            edge_recv.at[chunk],
            to_peer,
        )

    def mid_copy(h):
        return remote(own_mid.at[h], peer_mid.at[h], mid_send.at[h], mid_recv.at[h], to_peer)

    def back(way):
        return remote(
            back_src.at[way],
            back_dst.at[way],
            back_send.at[way],
            back_recv.at[way],
            to_upper if way == 0 else to_lower,
        )

    def each(low, high, action):
        def step(h, carry):
            action(h)
            return carry

        lax.fori_loop(low, high, step, 0)

    counts_load = pltpu.make_async_copy(counts_hbm, counts, counts_sem)
    counts_load.start()
    for array in range(3):
        raw_load(array).start()
    up_load.start()

    barrier = pltpu.get_barrier_semaphore()
    pl.semaphore_signal(barrier, inc=1, device_id=to_peer, device_id_type=MESH)

    @pl.when(core == 1)
    def _():
        for device in (to_upper, to_lower):
            pl.semaphore_signal(barrier, inc=1, device_id=device, device_id_type=MESH)
        pl.semaphore_wait(barrier, 1)

    @pl.when(core == 0)
    def _():
        pl.semaphore_wait(barrier, 3)

    for chunk in range(CHUNKS):
        do_copy(chunk).start()

    @pl.when(core == 0)
    def _():
        for device in (to_upper, to_lower):
            pl.semaphore_signal(ready, inc=1, device_id=device, device_id_type=MESH)

    counts_load.wait()
    plan = Plan(counts, groups)
    for array in range(3):
        raw_load(array).wait()

    def stage_move(h):
        for array in range(3):
            frame = raw[array, orig - 1, :, cols(h)]
            for slot in range(inner, orig - 1):
                frame = pick(plan.last_slot == slot, raw[array, slot, :, cols(h)], frame)
            move_src[array, :, cols(h)] = frame

    each(0, heads, stage_move)

    @pl.when(core == 1)
    def _():
        pl.semaphore_wait(ready, 2)

    move(1).start()
    move(0).start()

    def native_frame(h, array, slot):
        here = raw[array, slot, :, cols(h)]
        frame = pick(plan.shift == 1, raw[array, slot + 1, :, cols(h)], here)
        if slot > 0:
            frame = pick(plan.shift == -1, raw[array, slot - 1, :, cols(h)], frame)
        return frame

    def stage_mid(h):
        for array in range(3):
            for slot in range(inner):
                own_mid[h, array, slot] = native_frame(h, array, slot + 1)

    each(0, heads, stage_mid)

    def labels(dim):
        slot = (lax.broadcasted_iota(jnp.int32, (rows, rows), dim) // tokens) % dest
        low = jnp.where(slot == 0, plan.take_low, 0)
        high = jnp.where(slot == dest - 1, plan.take_high, 0)
        return high - low

    bias[...] = jnp.where(labels(0) == labels(1), 0.0, -jnp.inf)

    move(0).wait_recv()
    move(1).wait_recv()

    def stage_edge(h):
        for array in range(3):
            for way, (slot, moved) in enumerate(
                ((0, plan.from_low), (dest - 1, plan.from_high))
            ):
                frame = native_frame(h, array, slot)
                own_edge[h, array, way] = pick(moved, move_dst[way, array, :, cols(h)], frame)

    for chunk in range(CHUNKS):
        each(chunk * group_heads, (chunk + 1) * group_heads, stage_edge)
        edge_copy(chunk).start()

    def edge_up(h, way):
        slot, swap = ((0, plan.swap_low), (dest - 1, plan.swap_high))[way]
        mine, other = own_do[slot, :, cols(h)], peer_do[slot, :, cols(h)]
        return pick(swap, other, mine), pick(swap, mine, other)

    edge_row = lax.broadcasted_iota(jnp.int32, (4 * tokens, 4 * tokens), 0) // tokens % 2
    edge_col = lax.broadcasted_iota(jnp.int32, (4 * tokens, 4 * tokens), 1) // tokens % 2
    edge_mask = jnp.where(edge_row == edge_col, 0.0, -jnp.inf)

    def edge_compute(h):
        def joined(array):
            both = [ref[h, array].reshape(2 * tokens, HDIM) for ref in (own_edge, peer_edge)]
            return jnp.concatenate(both, axis=0)

        queries, keys, values = joined(0), joined(1), joined(2)
        (low, far_low), (high, far_high) = edge_up(h, 0), edge_up(h, 1)
        upstream = jnp.concatenate([low, high, far_low, far_high], axis=0)
        probs, logit_grad = attend(queries, keys, values, upstream, edge_mask)
        mine = 2 * tokens
        query_grad = dot(logit_grad[:mine], keys, ((1,), (0,))) * SCALING
        key_grad = dot(logit_grad[:, :mine], queries, ((0,), (0,))) * SCALING
        value_grad = dot(probs[:, :mine], upstream, ((0,), (0,)))
        for array, grad in enumerate((query_grad, key_grad, value_grad)):
            grad = grad.astype(jnp.bfloat16)
            back_src[1, h, array] = grad[:tokens]
            back_src[0, h, array] = grad[tokens:]

    def gather(h):
        edge = half - tokens
        for array in range(3):
            for base, edges, mids in ((0, own_edge, own_mid), (half, peer_edge, peer_mid)):
                cat[array, pl.ds(base, tokens)] = edges[h, array, 0]
                cat[array, pl.ds(base + tokens, edge - tokens)] = mids[h, array].reshape(
                    edge - tokens, HDIM
                )
                cat[array, pl.ds(base + edge, tokens)] = edges[h, array, 1]
        for slot in range(1, dest - 1):
            cat[3, pl.ds(slot * tokens, tokens)] = own_do[slot, :, cols(h)]
            cat[3, pl.ds(half + slot * tokens, tokens)] = peer_do[slot, :, cols(h)]
        for way, slot in enumerate(edge_slots):
            mine, other = edge_up(h, way)
            cat[3, pl.ds(slot * tokens, tokens)] = mine
            cat[3, pl.ds(half + slot * tokens, tokens)] = other

    def compute(h):
        results = attend_head(plan, (dest, tokens, HDIM), cat, bias, p_buf, ds_buf)
        o_out[:, :, cols(h)] = results[0]
        for array in range(3):
            grads[h, array] = results[array + 1]

    def assemble(h):
        for array in range(3):
            for slot in range(orig):
                (dq_out, dk_out, dv_out)[array][slot, :, cols(h)] = anchor_frame(
                    plan,
                    slot,
                    dest,
                    lambda index, array=array: grads[h, array, index],
                    back_dst[0, h, array],
                    back_dst[1, h, array],
                )

    up_load.wait()
    for chunk in range(CHUNKS):
        do_copy(chunk).wait_send()
    each(0, AHEAD, lambda h: mid_copy(h).start())
    for chunk in range(CHUNKS):
        do_copy(chunk).wait_recv()
    for chunk in range(CHUNKS):
        edge_copy(chunk).wait_recv()

        def edge_step(step, carry):
            for part in range(EDGE_UNROLL):
                edge_compute(step * EDGE_UNROLL + part)
            return carry

        count = group_heads // EDGE_UNROLL
        lax.fori_loop(chunk * count, (chunk + 1) * count, edge_step, 0)
    back(0).start()
    back(1).start()

    def main_step(h):
        @pl.when(h + AHEAD < heads)
        def _():
            mid_copy(h + AHEAD).start()

        mid_copy(h).wait_recv()
        gather(h)
        compute(h)

        @pl.when(h == GATHER_FROM)
        def _():
            back(0).wait_recv()
            back(1).wait_recv()
            each(0, GATHER_FROM, assemble)

        @pl.when(h >= GATHER_FROM)
        def _():
            assemble(h)

    each(0, heads - 1, main_step)
    last_back[...] = back_dst[:, heads - 1]
    for chunk in range(CHUNKS):
        edge_copy(chunk).wait_send()
    for way in range(2):
        move(way).wait_send()
        back(way).wait_send()
    each(0, heads, lambda h: mid_copy(h).wait_send())
    mid_copy(heads - 1).wait_recv()
    gather(heads - 1)


def store_kernel(
    groups,
    counts_hbm,
    o_in,
    dq_in,
    dk_in,
    dv_in,
    cat,
    bias,
    last_back,
    o_hbm,
    dq_hbm,
    dk_hbm,
    dv_hbm,
    counts,
    p_buf,
    ds_buf,
    o_last,
    g_last,
    counts_sem,
    store_sem,
    last_sem,
):
    dest, tokens, width = o_in.shape
    orig = dq_in.shape[0]
    early, late = pl.ds(0, width - HDIM), pl.ds(width - HDIM, HDIM)
    targets = (o_hbm, dq_hbm, dk_hbm, dv_hbm)
    counts_load = pltpu.make_async_copy(counts_hbm, counts, counts_sem)
    counts_load.start()
    stores = [
        pltpu.make_async_copy(
            source.at[:, :, early], target.at[:, :, early], store_sem.at[index]
        )
        for index, (source, target) in enumerate(zip((o_in, dq_in, dk_in, dv_in), targets))
    ]
    for store in stores:
        store.start()
    counts_load.wait()
    plan = Plan(counts, groups)
    results = attend_head(plan, (dest, tokens, HDIM), cat, bias, p_buf, ds_buf)
    o_last[...] = results[0]
    for array in range(3):
        for slot in range(orig):
            g_last[array, slot] = anchor_frame(
                plan,
                slot,
                dest,
                lambda index, array=array: results[array + 1][index],
                last_back[0, array],
                last_back[1, array],
            )
    lasts = [
        pltpu.make_async_copy(source, target.at[:, :, late], last_sem.at[index])
        for index, (source, target) in enumerate(
            zip((o_last, g_last.at[0], g_last.at[1], g_last.at[2]), targets)
        )
    ]
    for store in lasts:
        store.start()
    for store in stores + lasts:
        store.wait()


def body(query_frames, key_frames, value_frames, out_cotangent, frame_counts):
    groups = lax.axis_size("group")
    orig, tokens, width = query_frames.shape
    dest = out_cotangent.shape[0]
    heads = width // HDIM
    rows = 2 * dest * tokens
    bf16 = jnp.bfloat16
    anywhere = pl.BlockSpec(memory_space=pl.ANY)
    in_vmem = pl.BlockSpec(memory_space=pltpu.VMEM)
    anchor = (orig, tokens, width)
    attending = (dest, tokens, width)
    dma = pltpu.SemaphoreType.DMA
    shapes = (attending, anchor, anchor, anchor)
    counts = frame_counts.T
    results = pl.pallas_call(
        functools.partial(kernel, groups),
        out_shape=tuple(pltpu.VMEM(shape, bf16) for shape in shapes)
        + (
            pltpu.VMEM((4, rows, HDIM), bf16),
            pltpu.VMEM((rows, rows), jnp.float32),
            pltpu.VMEM((2, 3, tokens, HDIM), bf16),
        ),
        in_specs=[anywhere] * 5,
        out_specs=(in_vmem,) * 7,
        scratch_shapes=[
            pltpu.SMEM((3, groups), jnp.int32),
            pltpu.VMEM((3,) + anchor, bf16),
            pltpu.VMEM(attending, bf16),
            pltpu.VMEM(attending, bf16),
            pltpu.VMEM((heads, 3, 2, tokens, HDIM), bf16),
            pltpu.VMEM((heads, 3, 2, tokens, HDIM), bf16),
            pltpu.VMEM((heads, 3, dest - 2, tokens, HDIM), bf16),
            pltpu.VMEM((heads, 3, dest - 2, tokens, HDIM), bf16),
            pltpu.VMEM((3, tokens, width), bf16),
            pltpu.VMEM((2, 3, tokens, width), bf16),
            pltpu.VMEM((2, heads, 3, tokens, HDIM), bf16),
            pltpu.VMEM((2, heads, 3, tokens, HDIM), bf16),
            pltpu.VMEM((heads, 3, dest, tokens, HDIM), bf16),
            pltpu.VMEM((rows, rows), bf16),
            pltpu.VMEM((rows, rows), bf16),
            pltpu.SemaphoreType.REGULAR,
            dma,
            dma((3,)),
            dma,
            dma((2,)),
            dma((2,)),
            dma((CHUNKS,)),
            dma((CHUNKS,)),
            dma((CHUNKS,)),
            dma((CHUNKS,)),
            dma((heads,)),
            dma((heads,)),
            dma((2,)),
            dma((2,)),
        ],
        compiler_params=pltpu.CompilerParams(
            collective_id=0, has_side_effects=True, vmem_limit_bytes=54 << 20
        ),
    )(counts, query_frames, key_frames, value_frames, out_cotangent)
    return pl.pallas_call(
        functools.partial(store_kernel, groups),
        out_shape=tuple(jax.ShapeDtypeStruct(shape, bf16) for shape in shapes),
        in_specs=[anywhere] + [in_vmem] * 7,
        out_specs=(anywhere,) * 4,
        scratch_shapes=[
            pltpu.SMEM((3, groups), jnp.int32),
            pltpu.VMEM((rows, rows), bf16),
            pltpu.VMEM((rows, rows), bf16),
            pltpu.VMEM((dest, tokens, HDIM), bf16),
            pltpu.VMEM((3, orig, tokens, HDIM), bf16),
            dma,
            dma((4,)),
            dma((4,)),
        ],
        compiler_params=pltpu.CompilerParams(vmem_limit_bytes=16 << 20),
    )(counts, *results)


def solution(mesh):
    spread = P("group", "sp", None)
    return jax.shard_map(
        body,
        mesh=mesh,
        in_specs=(spread, spread, spread, spread, P()),
        out_specs=(spread,) * 4,
        check_vma=False,
    )
```

```python
import functools
import math

import jax
import jax.numpy as jnp
from jax import lax
from jax.experimental import pallas as pl
from jax.experimental.pallas import tpu as pltpu
from jax.sharding import PartitionSpec as P

HDIM = 128
SCALING = 1.0 / math.sqrt(HDIM)
EXPONENT = SCALING * math.log2(math.e)
MESH = pl.DeviceIdType.MESH
CHUNKS = 2
AHEAD = 2
PAIRS = 8
EDGE_UNROLL = 5
GATHER_FROM = 14
ROW_BLOCKS = 4


def pick(cond, yes, no):
    return lax.select_n(cond, no, yes)


def dot(left, right, dims):
    return lax.dot_general(left, right, (dims, ((), ())), preferred_element_type=jnp.float32)


def attend(queries, keys, values, upstream, mask):
    logits = dot(queries, keys, ((1,), (1,))) * EXPONENT + mask
    powers = jnp.exp2(logits - jnp.max(logits, axis=1, keepdims=True))
    softmax = powers * (1.0 / jnp.sum(powers, axis=1, keepdims=True))
    prob_grad = dot(upstream, values, ((1,), (1,)))
    correction = jnp.sum(softmax * prob_grad, axis=1, keepdims=True)
    logit_grad = softmax * (prob_grad - correction)
    return softmax.astype(jnp.bfloat16), logit_grad.astype(jnp.bfloat16)


def attend_head(plan, shape, cat, bias, p_buf, ds_buf):
    tokens = shape[1]
    rows = cat.shape[1]
    half = rows // 2
    edge = half - tokens
    size = rows // ROW_BLOCKS
    for block in range(ROW_BLOCKS):
        span = pl.ds(block * size, size)
        p_buf[span], ds_buf[span] = attend(cat[0, span], cat[1], cat[2], cat[3, span], bias[span])
    probs = jnp.concatenate(
        [
            pick(plan.swap_low, p_buf[half : half + tokens], p_buf[:tokens]),
            p_buf[tokens:edge],
            pick(plan.swap_high, p_buf[half + edge :], p_buf[edge:half]),
        ],
        axis=0,
    )
    attended = dot(probs, cat[2], ((1,), (0,)))
    query_grad = dot(ds_buf[:half], cat[1], ((1,), (0,))) * SCALING
    key_grad = dot(ds_buf[:, :half], cat[0], ((0,), (0,))) * SCALING
    value_grad = dot(p_buf[:, :half], cat[3], ((0,), (0,)))
    results = (attended, query_grad, key_grad, value_grad)
    return [result.astype(jnp.bfloat16).reshape(shape) for result in results]


class Plan:
    def __init__(self, counts, groups):
        g = lax.axis_index("group")
        core = g % 2
        upper = (g + 1) % groups
        lower = (g + groups - 1) % groups
        self.take_low = counts[0, g]
        self.take_high = counts[2, g]
        self.give_low = counts[2, lower]
        self.give_high = counts[0, upper]
        self.shift = self.give_low - self.take_low
        self.last_slot = self.give_low + counts[1, g]
        self.from_low = self.take_low == 1
        self.from_high = self.take_high == 1
        self.swap_low = jnp.logical_and(core == 0, self.from_low)
        self.swap_high = jnp.logical_and(core == 1, self.from_high)


def anchor_frame(plan, slot, dest, grad, low_back, high_back):
    zero = jnp.zeros_like(low_back)

    def source(index):
        return grad(index) if 0 <= index < dest else zero

    frame = pick(plan.shift == 1, source(slot - 1), source(slot))
    frame = pick(plan.shift == -1, source(slot + 1), frame)
    inside = jnp.logical_and(slot >= plan.give_low, slot < plan.last_slot)
    frame = pick(inside, frame, zero)
    if slot == 0:
        frame = pick(plan.give_low == 1, low_back, frame)
    if slot >= dest - 2:
        top = jnp.logical_and(plan.last_slot == slot, plan.give_high == 1)
        frame = pick(top, high_back, frame)
    return frame


def kernel(
    groups,
    counts_hbm,
    q_hbm,
    k_hbm,
    v_hbm,
    do_hbm,
    o_out,
    dq_out,
    dk_out,
    dv_out,
    cat,
    bias,
    last_back,
    counts,
    raw,
    own_do,
    peer_do,
    own_edge,
    peer_edge,
    own_mid,
    peer_mid,
    move_src,
    move_dst,
    back_src,
    back_dst,
    grads,
    p_buf,
    ds_buf,
    ready,
    counts_sem,
    raw_sem,
    up_sem,
    move_send,
    move_recv,
    do_send,
    do_recv,
    edge_send,
    edge_recv,
    mid_send,
    mid_recv,
    back_send,
    back_recv,
):
    heads = own_mid.shape[0]
    dest, tokens, _ = own_do.shape
    orig = raw.shape[1]
    inner = dest - 2
    half = dest * tokens
    rows = 2 * half
    edge_slots = (0, dest - 1)
    group_heads = heads // CHUNKS

    g = lax.axis_index("group")
    s = lax.axis_index("sp")
    core = g % 2
    upper = (g + 1) % groups
    lower = (g + groups - 1) % groups
    flip = 1 - 2 * s
    to_peer = {"group": g, "sp": 1 - s}
    to_upper = {"group": upper, "sp": s + core * flip}
    to_lower = {"group": lower, "sp": s + (1 - core) * flip}

    def cols(h):
        return pl.ds(pl.multiple_of(h * HDIM, HDIM), HDIM)

    def raw_load(array):
        source = (q_hbm, k_hbm, v_hbm)[array]
        return pltpu.make_async_copy(source, raw.at[array], raw_sem.at[array])

    up_load = pltpu.make_async_copy(do_hbm, own_do, up_sem)

    def remote(src, dst, send, recv, device):
        return pltpu.make_async_remote_copy(
            src_ref=src,
            dst_ref=dst,
            send_sem=send,
            recv_sem=recv,
            device_id=device,
            device_id_type=MESH,
        )

    def move(way):
        source = move_src if way == 0 else raw.at[:, 0]
        return remote(
            source,
            move_dst.at[way],
            move_send.at[way],
            move_recv.at[way],
            to_upper if way == 0 else to_lower,
        )

    do_copy = remote(do_hbm, peer_do, do_send, do_recv, to_peer)

    def edge_copy(chunk):
        span = pl.ds(chunk * group_heads, group_heads)
        return remote(
            own_edge.at[span],
            peer_edge.at[span],
            edge_send.at[chunk],
            edge_recv.at[chunk],
            to_peer,
        )

    def mid_copy(h):
        return remote(own_mid.at[h], peer_mid.at[h], mid_send.at[h], mid_recv.at[h], to_peer)

    def pair_copy(pair):
        span, h = pl.ds(2 * pair, 2), 2 * pair
        return remote(own_mid.at[span], peer_mid.at[span], mid_send.at[h], mid_recv.at[h], to_peer)

    def back(way):
        return remote(
            back_src.at[way],
            back_dst.at[way],
            back_send.at[way],
            back_recv.at[way],
            to_upper if way == 0 else to_lower,
        )

    def each(low, high, action):
        def step(h, carry):
            action(h)
            return carry

        lax.fori_loop(low, high, step, 0)

    barrier = pltpu.get_barrier_semaphore()
    pl.semaphore_signal(barrier, inc=1, device_id=to_peer, device_id_type=MESH)

    @pl.when(core == 1)
    def _():
        for device in (to_upper, to_lower):
            pl.semaphore_signal(barrier, inc=1, device_id=device, device_id_type=MESH)

    counts_load = pltpu.make_async_copy(counts_hbm, counts, counts_sem)
    counts_load.start()
    for array in range(3):
        raw_load(array).start()
    up_load.start()

    @pl.when(core == 1)
    def _():
        pl.semaphore_wait(barrier, 1)

    @pl.when(core == 0)
    def _():
        pl.semaphore_wait(barrier, 3)

    do_copy.start()

    @pl.when(core == 0)
    def _():
        for device in (to_upper, to_lower):
            pl.semaphore_signal(ready, inc=1, device_id=device, device_id_type=MESH)

    counts_load.wait()
    plan = Plan(counts, groups)
    for array in range(3):
        raw_load(array).wait()

    def stage_move(h):
        for array in range(3):
            frame = raw[array, orig - 1, :, cols(h)]
            for slot in range(inner, orig - 1):
                frame = pick(plan.last_slot == slot, raw[array, slot, :, cols(h)], frame)
            move_src[array, :, cols(h)] = frame

    each(0, heads, stage_move)

    @pl.when(core == 1)
    def _():
        pl.semaphore_wait(ready, 2)

    move(1).start()
    move(0).start()

    def native_frame(h, array, slot):
        here = raw[array, slot, :, cols(h)]
        frame = pick(plan.shift == 1, raw[array, slot + 1, :, cols(h)], here)
        if slot > 0:
            frame = pick(plan.shift == -1, raw[array, slot - 1, :, cols(h)], frame)
        return frame

    def stage_mid(h):
        for array in range(3):
            for slot in range(inner):
                own_mid[h, array, slot] = native_frame(h, array, slot + 1)

    each(0, heads, stage_mid)

    def labels(dim):
        slot = (lax.broadcasted_iota(jnp.int32, (rows, rows), dim) // tokens) % dest
        low = jnp.where(slot == 0, plan.take_low, 0)
        high = jnp.where(slot == dest - 1, plan.take_high, 0)
        return high - low

    bias[...] = jnp.where(labels(0) == labels(1), 0.0, -jnp.inf)

    move(0).wait_recv()
    move(1).wait_recv()

    def stage_edge(h):
        for array in range(3):
            for way, (slot, moved) in enumerate(
                ((0, plan.from_low), (dest - 1, plan.from_high))
            ):
                frame = native_frame(h, array, slot)
                own_edge[h, array, way] = pick(moved, move_dst[way, array, :, cols(h)], frame)

    for chunk in range(CHUNKS):
        each(chunk * group_heads, (chunk + 1) * group_heads, stage_edge)
        edge_copy(chunk).start()

    def edge_up(h, way):
        slot, swap = ((0, plan.swap_low), (dest - 1, plan.swap_high))[way]
        mine, other = own_do[slot, :, cols(h)], peer_do[slot, :, cols(h)]
        return pick(swap, other, mine), pick(swap, mine, other)

    edge_row = lax.broadcasted_iota(jnp.int32, (4 * tokens, 4 * tokens), 0) // tokens % 2
    edge_col = lax.broadcasted_iota(jnp.int32, (4 * tokens, 4 * tokens), 1) // tokens % 2
    edge_mask = jnp.where(edge_row == edge_col, 0.0, -jnp.inf)

    def edge_compute(h):
        def joined(array):
            both = [ref[h, array].reshape(2 * tokens, HDIM) for ref in (own_edge, peer_edge)]
            return jnp.concatenate(both, axis=0)

        queries, keys, values = joined(0), joined(1), joined(2)
        (low, far_low), (high, far_high) = edge_up(h, 0), edge_up(h, 1)
        upstream = jnp.concatenate([low, high, far_low, far_high], axis=0)
        probs, logit_grad = attend(queries, keys, values, upstream, edge_mask)
        mine = 2 * tokens
        query_grad = dot(logit_grad[:mine], keys, ((1,), (0,))) * SCALING
        key_grad = dot(logit_grad[:, :mine], queries, ((0,), (0,))) * SCALING
        value_grad = dot(probs[:, :mine], upstream, ((0,), (0,)))
        for array, grad in enumerate((query_grad, key_grad, value_grad)):
            grad = grad.astype(jnp.bfloat16)
            back_src[1, h, array] = grad[:tokens]
            back_src[0, h, array] = grad[tokens:]

    def gather_mid(h, base, mids):
        for array in range(3):
            cat[array, pl.ds(base + tokens, inner * tokens)] = mids[h, array].reshape(
                inner * tokens, HDIM
            )

    def gather(h):
        edge = half - tokens
        gather_mid(h, 0, own_mid)
        for array in range(3):
            for base, edges in ((0, own_edge), (half, peer_edge)):
                cat[array, pl.ds(base, tokens)] = edges[h, array, 0]
                cat[array, pl.ds(base + edge, tokens)] = edges[h, array, 1]
        for slot in range(1, dest - 1):
            cat[3, pl.ds(slot * tokens, tokens)] = own_do[slot, :, cols(h)]
            cat[3, pl.ds(half + slot * tokens, tokens)] = peer_do[slot, :, cols(h)]
        for way, slot in enumerate(edge_slots):
            mine, other = edge_up(h, way)
            cat[3, pl.ds(slot * tokens, tokens)] = mine
            cat[3, pl.ds(half + slot * tokens, tokens)] = other

    def compute(h):
        results = attend_head(plan, (dest, tokens, HDIM), cat, bias, p_buf, ds_buf)
        o_out[:, :, cols(h)] = results[0]
        for array in range(3):
            grads[h, array] = results[array + 1]

    def assemble(h):
        for array in range(3):
            for slot in range(orig):
                (dq_out, dk_out, dv_out)[array][slot, :, cols(h)] = anchor_frame(
                    plan,
                    slot,
                    dest,
                    lambda index, array=array: grads[h, array, index],
                    back_dst[0, h, array],
                    back_dst[1, h, array],
                )

    up_load.wait()
    do_copy.wait_send()
    each(0, AHEAD, lambda pair: pair_copy(pair).start())
    do_copy.wait_recv()
    for chunk in range(CHUNKS):
        edge_copy(chunk).wait_recv()

        def edge_step(step, carry):
            for part in range(EDGE_UNROLL):
                edge_compute(step * EDGE_UNROLL + part)
            return carry

        count = group_heads // EDGE_UNROLL
        lax.fori_loop(chunk * count, (chunk + 1) * count, edge_step, 0)
    back(0).start()
    back(1).start()

    def main_step(h):
        gather(h)

        @pl.when(jnp.logical_and(h < 2 * PAIRS, h % 2 == 0))
        def _():
            pair = h // 2

            @pl.when(pair + AHEAD < PAIRS)
            def _():
                pair_copy(pair + AHEAD).start()

            pair_copy(pair).wait_recv()

        @pl.when(h == 2 * PAIRS - 6)
        def _():
            each(2 * PAIRS, heads, lambda late: mid_copy(late).start())

        @pl.when(h >= 2 * PAIRS)
        def _():
            mid_copy(h).wait_recv()

        gather_mid(h, half, peer_mid)
        compute(h)

        @pl.when(h == GATHER_FROM)
        def _():
            back(0).wait_recv()
            back(1).wait_recv()
            each(0, GATHER_FROM, assemble)

        @pl.when(h >= GATHER_FROM)
        def _():
            assemble(h)

    each(0, heads - 1, main_step)
    last_back[...] = back_dst[:, heads - 1]
    gather(heads - 1)
    for chunk in range(CHUNKS):
        edge_copy(chunk).wait_send()
    for way in range(2):
        move(way).wait_send()
        back(way).wait_send()
    each(0, PAIRS, lambda pair: pair_copy(pair).wait_send())
    each(2 * PAIRS, heads, lambda h: mid_copy(h).wait_send())
    mid_copy(heads - 1).wait_recv()
    gather_mid(heads - 1, half, peer_mid)


def store_kernel(
    groups,
    counts_hbm,
    o_in,
    dq_in,
    dk_in,
    dv_in,
    cat,
    bias,
    last_back,
    o_hbm,
    dq_hbm,
    dk_hbm,
    dv_hbm,
    counts,
    p_buf,
    ds_buf,
    o_last,
    g_last,
    counts_sem,
    store_sem,
    last_sem,
):
    dest, tokens, width = o_in.shape
    orig = dq_in.shape[0]
    early, late = pl.ds(0, width - HDIM), pl.ds(width - HDIM, HDIM)
    targets = (o_hbm, dq_hbm, dk_hbm, dv_hbm)
    counts_load = pltpu.make_async_copy(counts_hbm, counts, counts_sem)
    counts_load.start()
    stores = [
        pltpu.make_async_copy(
            source.at[:, :, early], target.at[:, :, early], store_sem.at[index]
        )
        for index, (source, target) in enumerate(zip((o_in, dq_in, dk_in, dv_in), targets))
    ]
    for store in stores:
        store.start()
    counts_load.wait()
    plan = Plan(counts, groups)
    results = attend_head(plan, (dest, tokens, HDIM), cat, bias, p_buf, ds_buf)
    o_last[...] = results[0]
    for array in range(3):
        for slot in range(orig):
            g_last[array, slot] = anchor_frame(
                plan,
                slot,
                dest,
                lambda index, array=array: results[array + 1][index],
                last_back[0, array],
                last_back[1, array],
            )
    lasts = [
        pltpu.make_async_copy(source, target.at[:, :, late], last_sem.at[index])
        for index, (source, target) in enumerate(
            zip((o_last, g_last.at[0], g_last.at[1], g_last.at[2]), targets)
        )
    ]
    for store in lasts:
        store.start()
    for store in stores + lasts:
        store.wait()


def body(query_frames, key_frames, value_frames, out_cotangent, frame_counts):
    groups = lax.axis_size("group")
    orig, tokens, width = query_frames.shape
    dest = out_cotangent.shape[0]
    heads = width // HDIM
    rows = 2 * dest * tokens
    bf16 = jnp.bfloat16
    anywhere = pl.BlockSpec(memory_space=pl.ANY)
    in_vmem = pl.BlockSpec(memory_space=pltpu.VMEM)
    anchor = (orig, tokens, width)
    attending = (dest, tokens, width)
    dma = pltpu.SemaphoreType.DMA
    shapes = (attending, anchor, anchor, anchor)
    counts = frame_counts.T
    results = pl.pallas_call(
        functools.partial(kernel, groups),
        out_shape=tuple(pltpu.VMEM(shape, bf16) for shape in shapes)
        + (
            pltpu.VMEM((4, rows, HDIM), bf16),
            pltpu.VMEM((rows, rows), jnp.float32),
            pltpu.VMEM((2, 3, tokens, HDIM), bf16),
        ),
        in_specs=[anywhere] * 5,
        out_specs=(in_vmem,) * 7,
        scratch_shapes=[
            pltpu.SMEM((3, groups), jnp.int32),
            pltpu.VMEM((3,) + anchor, bf16),
            pltpu.VMEM(attending, bf16),
            pltpu.VMEM(attending, bf16),
            pltpu.VMEM((heads, 3, 2, tokens, HDIM), bf16),
            pltpu.VMEM((heads, 3, 2, tokens, HDIM), bf16),
            pltpu.VMEM((heads, 3, dest - 2, tokens, HDIM), bf16),
            pltpu.VMEM((heads, 3, dest - 2, tokens, HDIM), bf16),
            pltpu.VMEM((3, tokens, width), bf16),
            pltpu.VMEM((2, 3, tokens, width), bf16),
            pltpu.VMEM((2, heads, 3, tokens, HDIM), bf16),
            pltpu.VMEM((2, heads, 3, tokens, HDIM), bf16),
            pltpu.VMEM((heads, 3, dest, tokens, HDIM), bf16),
            pltpu.VMEM((rows, rows), bf16),
            pltpu.VMEM((rows, rows), bf16),
            pltpu.SemaphoreType.REGULAR,
            dma,
            dma((3,)),
            dma,
            dma((2,)),
            dma((2,)),
            dma,
            dma,
            dma((CHUNKS,)),
            dma((CHUNKS,)),
            dma((heads,)),
            dma((heads,)),
            dma((2,)),
            dma((2,)),
        ],
        compiler_params=pltpu.CompilerParams(
            collective_id=0, has_side_effects=True, vmem_limit_bytes=54 << 20
        ),
    )(counts, query_frames, key_frames, value_frames, out_cotangent)
    return pl.pallas_call(
        functools.partial(store_kernel, groups),
        out_shape=tuple(jax.ShapeDtypeStruct(shape, bf16) for shape in shapes),
        in_specs=[anywhere] + [in_vmem] * 7,
        out_specs=(anywhere,) * 4,
        scratch_shapes=[
            pltpu.SMEM((3, groups), jnp.int32),
            pltpu.VMEM((rows, rows), bf16),
            pltpu.VMEM((rows, rows), bf16),
            pltpu.VMEM((dest, tokens, HDIM), bf16),
            pltpu.VMEM((3, orig, tokens, HDIM), bf16),
            dma,
            dma((4,)),
            dma((4,)),
        ],
        compiler_params=pltpu.CompilerParams(vmem_limit_bytes=16 << 20),
    )(counts, *results)


def solution(mesh):
    spread = P("group", "sp", None)
    return jax.shard_map(
        body,
        mesh=mesh,
        in_specs=(spread, spread, spread, spread, P()),
        out_specs=(spread,) * 4,
        check_vma=False,
    )
```

```python
import functools
import math

import jax
import jax.numpy as jnp
from jax import lax
from jax.experimental import pallas as pl
from jax.experimental.pallas import tpu as pltpu
from jax.sharding import PartitionSpec as P

HDIM = 128
SCALING = 1.0 / math.sqrt(HDIM)
EXPONENT = SCALING * math.log2(math.e)
MESH = pl.DeviceIdType.MESH
CHUNKS = 2
AHEAD = 2
PAIRS = 8
EDGE_UNROLL = 5
GATHER_FROM = 8
ROW_BLOCKS = 4


def pick(cond, yes, no):
    return lax.select_n(cond, no, yes)


def dot(left, right, dims):
    return lax.dot_general(left, right, (dims, ((), ())), preferred_element_type=jnp.float32)


def attend(queries, keys, values, upstream, mask):
    logits = dot(queries, keys, ((1,), (1,))) * EXPONENT + mask
    powers = jnp.exp2(logits - jnp.max(logits, axis=1, keepdims=True))
    softmax = powers * (1.0 / jnp.sum(powers, axis=1, keepdims=True))
    prob_grad = dot(upstream, values, ((1,), (1,)))
    correction = jnp.sum(softmax * prob_grad, axis=1, keepdims=True)
    logit_grad = softmax * (prob_grad - correction)
    return softmax.astype(jnp.bfloat16), logit_grad.astype(jnp.bfloat16)


def attend_head(plan, shape, cat, bias, p_buf, ds_buf):
    tokens = shape[1]
    rows = cat.shape[1]
    half = rows // 2
    edge = half - tokens
    size = rows // ROW_BLOCKS
    for block in range(ROW_BLOCKS):
        span = pl.ds(block * size, size)
        p_buf[span], ds_buf[span] = attend(cat[0, span], cat[1], cat[2], cat[3, span], bias[span])
    probs = jnp.concatenate(
        [
            pick(plan.swap_low, p_buf[half : half + tokens], p_buf[:tokens]),
            p_buf[tokens:edge],
            pick(plan.swap_high, p_buf[half + edge :], p_buf[edge:half]),
        ],
        axis=0,
    )
    attended = dot(probs, cat[2], ((1,), (0,)))
    query_grad = dot(ds_buf[:half], cat[1], ((1,), (0,))) * SCALING
    key_grad = dot(ds_buf[:, :half], cat[0], ((0,), (0,))) * SCALING
    value_grad = dot(p_buf[:, :half], cat[3], ((0,), (0,)))
    results = (attended, query_grad, key_grad, value_grad)
    return [result.astype(jnp.bfloat16).reshape(shape) for result in results]


class Plan:
    def __init__(self, counts, groups):
        g = lax.axis_index("group")
        core = g % 2
        upper = (g + 1) % groups
        lower = (g + groups - 1) % groups
        self.take_low = counts[0, g]
        self.take_high = counts[2, g]
        self.give_low = counts[2, lower]
        self.give_high = counts[0, upper]
        self.shift = self.give_low - self.take_low
        self.last_slot = self.give_low + counts[1, g]
        self.from_low = self.take_low == 1
        self.from_high = self.take_high == 1
        self.swap_low = jnp.logical_and(core == 0, self.from_low)
        self.swap_high = jnp.logical_and(core == 1, self.from_high)


def anchor_frame(plan, slot, dest, grad, low_back, high_back):
    zero = jnp.zeros_like(low_back)

    def source(index):
        return grad(index) if 0 <= index < dest else zero

    frame = pick(plan.shift == 1, source(slot - 1), source(slot))
    frame = pick(plan.shift == -1, source(slot + 1), frame)
    inside = jnp.logical_and(slot >= plan.give_low, slot < plan.last_slot)
    frame = pick(inside, frame, zero)
    if slot == 0:
        frame = pick(plan.give_low == 1, low_back, frame)
    if slot >= dest - 2:
        top = jnp.logical_and(plan.last_slot == slot, plan.give_high == 1)
        frame = pick(top, high_back, frame)
    return frame


def kernel(
    groups,
    counts_hbm,
    q_hbm,
    k_hbm,
    v_hbm,
    do_hbm,
    o_out,
    dq_out,
    dk_out,
    dv_out,
    cat,
    bias,
    last_back,
    counts,
    raw,
    own_do,
    peer_do,
    own_edge,
    peer_edge,
    own_mid,
    peer_mid,
    move_src,
    move_dst,
    back_src,
    back_dst,
    grads,
    p_buf,
    ds_buf,
    ready,
    counts_sem,
    raw_sem,
    up_sem,
    move_send,
    move_recv,
    do_send,
    do_recv,
    edge_send,
    edge_recv,
    mid_send,
    mid_recv,
    back_send,
    back_recv,
):
    heads = own_mid.shape[0]
    dest, tokens, _ = own_do.shape
    orig = raw.shape[1]
    inner = dest - 2
    half = dest * tokens
    rows = 2 * half
    edge_slots = (0, dest - 1)
    group_heads = heads // CHUNKS

    g = lax.axis_index("group")
    s = lax.axis_index("sp")
    core = g % 2
    upper = (g + 1) % groups
    lower = (g + groups - 1) % groups
    flip = 1 - 2 * s
    to_peer = {"group": g, "sp": 1 - s}
    to_upper = {"group": upper, "sp": s + core * flip}
    to_lower = {"group": lower, "sp": s + (1 - core) * flip}

    def cols(h):
        return pl.ds(pl.multiple_of(h * HDIM, HDIM), HDIM)

    def raw_load(array):
        source = (q_hbm, k_hbm, v_hbm)[array]
        return pltpu.make_async_copy(source, raw.at[array], raw_sem.at[array])

    up_load = pltpu.make_async_copy(do_hbm, own_do, up_sem)

    def remote(src, dst, send, recv, device):
        return pltpu.make_async_remote_copy(
            src_ref=src,
            dst_ref=dst,
            send_sem=send,
            recv_sem=recv,
            device_id=device,
            device_id_type=MESH,
        )

    def move(way):
        source = move_src if way == 0 else raw.at[:, 0]
        return remote(
            source,
            move_dst.at[way],
            move_send.at[way],
            move_recv.at[way],
            to_upper if way == 0 else to_lower,
        )

    do_copy = remote(do_hbm, peer_do, do_send, do_recv, to_peer)

    def edge_copy(chunk):
        span = pl.ds(chunk * group_heads, group_heads)
        return remote(
            own_edge.at[span],
            peer_edge.at[span],
            edge_send.at[chunk],
            edge_recv.at[chunk],
            to_peer,
        )

    def mid_copy(h):
        return remote(own_mid.at[h], peer_mid.at[h], mid_send.at[h], mid_recv.at[h], to_peer)

    def pair_copy(pair):
        span, h = pl.ds(2 * pair, 2), 2 * pair
        return remote(own_mid.at[span], peer_mid.at[span], mid_send.at[h], mid_recv.at[h], to_peer)

    def back(way):
        return remote(
            back_src.at[way],
            back_dst.at[way],
            back_send.at[way],
            back_recv.at[way],
            to_upper if way == 0 else to_lower,
        )

    def each(low, high, action):
        def step(h, carry):
            action(h)
            return carry

        lax.fori_loop(low, high, step, 0)

    barrier = pltpu.get_barrier_semaphore()
    pl.semaphore_signal(barrier, inc=1, device_id=to_peer, device_id_type=MESH)

    @pl.when(core == 1)
    def _():
        for device in (to_upper, to_lower):
            pl.semaphore_signal(barrier, inc=1, device_id=device, device_id_type=MESH)

    counts_load = pltpu.make_async_copy(counts_hbm, counts, counts_sem)
    counts_load.start()
    for array in range(3):
        raw_load(array).start()
    up_load.start()

    @pl.when(core == 1)
    def _():
        pl.semaphore_wait(barrier, 1)

    @pl.when(core == 0)
    def _():
        pl.semaphore_wait(barrier, 3)

    do_copy.start()

    @pl.when(core == 0)
    def _():
        for device in (to_upper, to_lower):
            pl.semaphore_signal(ready, inc=1, device_id=device, device_id_type=MESH)

    counts_load.wait()
    plan = Plan(counts, groups)
    for array in range(3):
        raw_load(array).wait()

    def stage_move(h):
        for array in range(3):
            frame = raw[array, orig - 1, :, cols(h)]
            for slot in range(inner, orig - 1):
                frame = pick(plan.last_slot == slot, raw[array, slot, :, cols(h)], frame)
            move_src[array, :, cols(h)] = frame

    each(0, heads, stage_move)

    @pl.when(core == 1)
    def _():
        pl.semaphore_wait(ready, 2)

    move(1).start()
    move(0).start()

    def native_frame(h, array, slot):
        here = raw[array, slot, :, cols(h)]
        frame = pick(plan.shift == 1, raw[array, slot + 1, :, cols(h)], here)
        if slot > 0:
            frame = pick(plan.shift == -1, raw[array, slot - 1, :, cols(h)], frame)
        return frame

    def stage_mid(h):
        for array in range(3):
            for slot in range(inner):
                own_mid[h, array, slot] = native_frame(h, array, slot + 1)

    each(0, heads, stage_mid)

    def labels(dim):
        slot = (lax.broadcasted_iota(jnp.int32, (rows, rows), dim) // tokens) % dest
        low = jnp.where(slot == 0, plan.take_low, 0)
        high = jnp.where(slot == dest - 1, plan.take_high, 0)
        return high - low

    bias[...] = jnp.where(labels(0) == labels(1), 0.0, -jnp.inf)

    move(0).wait_recv()
    move(1).wait_recv()

    def stage_edge(h):
        for array in range(3):
            for way, (slot, moved) in enumerate(
                ((0, plan.from_low), (dest - 1, plan.from_high))
            ):
                frame = native_frame(h, array, slot)
                own_edge[h, array, way] = pick(moved, move_dst[way, array, :, cols(h)], frame)

    for chunk in range(CHUNKS):
        each(chunk * group_heads, (chunk + 1) * group_heads, stage_edge)
        edge_copy(chunk).start()

    def edge_up(h, way):
        slot, swap = ((0, plan.swap_low), (dest - 1, plan.swap_high))[way]
        mine, other = own_do[slot, :, cols(h)], peer_do[slot, :, cols(h)]
        return pick(swap, other, mine), pick(swap, mine, other)

    edge_row = lax.broadcasted_iota(jnp.int32, (4 * tokens, 4 * tokens), 0) // tokens % 2
    edge_col = lax.broadcasted_iota(jnp.int32, (4 * tokens, 4 * tokens), 1) // tokens % 2
    edge_mask = jnp.where(edge_row == edge_col, 0.0, -jnp.inf)

    def edge_compute(h):
        def joined(array):
            both = [ref[h, array].reshape(2 * tokens, HDIM) for ref in (own_edge, peer_edge)]
            return jnp.concatenate(both, axis=0)

        queries, keys, values = joined(0), joined(1), joined(2)
        (low, far_low), (high, far_high) = edge_up(h, 0), edge_up(h, 1)
        upstream = jnp.concatenate([low, high, far_low, far_high], axis=0)
        probs, logit_grad = attend(queries, keys, values, upstream, edge_mask)
        mine = 2 * tokens
        query_grad = dot(logit_grad[:mine], keys, ((1,), (0,))) * SCALING
        key_grad = dot(logit_grad[:, :mine], queries, ((0,), (0,))) * SCALING
        value_grad = dot(probs[:, :mine], upstream, ((0,), (0,)))
        for array, grad in enumerate((query_grad, key_grad, value_grad)):
            grad = grad.astype(jnp.bfloat16)
            back_src[1, h, array] = grad[:tokens]
            back_src[0, h, array] = grad[tokens:]

    def gather_mid(h, base, mids):
        for array in range(3):
            cat[array, pl.ds(base + tokens, inner * tokens)] = mids[h, array].reshape(
                inner * tokens, HDIM
            )

    def gather(h):
        edge = half - tokens
        gather_mid(h, 0, own_mid)
        for array in range(3):
            for base, edges in ((0, own_edge), (half, peer_edge)):
                cat[array, pl.ds(base, tokens)] = edges[h, array, 0]
                cat[array, pl.ds(base + edge, tokens)] = edges[h, array, 1]
        for slot in range(1, dest - 1):
            cat[3, pl.ds(slot * tokens, tokens)] = own_do[slot, :, cols(h)]
            cat[3, pl.ds(half + slot * tokens, tokens)] = peer_do[slot, :, cols(h)]
        for way, slot in enumerate(edge_slots):
            mine, other = edge_up(h, way)
            cat[3, pl.ds(slot * tokens, tokens)] = mine
            cat[3, pl.ds(half + slot * tokens, tokens)] = other

    def compute(h):
        results = attend_head(plan, (dest, tokens, HDIM), cat, bias, p_buf, ds_buf)
        o_out[:, :, cols(h)] = results[0]
        for array in range(3):
            grads[h, array] = results[array + 1]

    def assemble(h):
        for array in range(3):
            for slot in range(orig):
                (dq_out, dk_out, dv_out)[array][slot, :, cols(h)] = anchor_frame(
                    plan,
                    slot,
                    dest,
                    lambda index, array=array: grads[h, array, index],
                    back_dst[0, h, array],
                    back_dst[1, h, array],
                )

    up_load.wait()
    do_copy.wait_send()
    each(0, AHEAD, lambda pair: pair_copy(pair).start())
    do_copy.wait_recv()
    for chunk in range(CHUNKS):
        edge_copy(chunk).wait_recv()

        def edge_step(step, carry):
            for part in range(EDGE_UNROLL):
                edge_compute(step * EDGE_UNROLL + part)
            return carry

        count = group_heads // EDGE_UNROLL
        lax.fori_loop(chunk * count, (chunk + 1) * count, edge_step, 0)
    back(0).start()
    back(1).start()

    def main_step(h):
        gather(h)

        @pl.when(jnp.logical_and(h < 2 * PAIRS, h % 2 == 0))
        def _():
            pair = h // 2

            @pl.when(pair + AHEAD < PAIRS)
            def _():
                pair_copy(pair + AHEAD).start()

            pair_copy(pair).wait_recv()

        @pl.when(h == 2 * PAIRS - 6)
        def _():
            each(2 * PAIRS, heads, lambda late: mid_copy(late).start())

        @pl.when(h >= 2 * PAIRS)
        def _():
            mid_copy(h).wait_recv()

        gather_mid(h, half, peer_mid)
        compute(h)

        @pl.when(h == GATHER_FROM)
        def _():
            back(0).wait_recv()
            back(1).wait_recv()
            each(0, GATHER_FROM, assemble)

        @pl.when(h >= GATHER_FROM)
        def _():
            assemble(h)

    each(0, heads - 1, main_step)
    last_back[...] = back_dst[:, heads - 1]
    gather(heads - 1)
    for chunk in range(CHUNKS):
        edge_copy(chunk).wait_send()
    for way in range(2):
        move(way).wait_send()
        back(way).wait_send()
    each(0, PAIRS, lambda pair: pair_copy(pair).wait_send())
    each(2 * PAIRS, heads, lambda h: mid_copy(h).wait_send())
    mid_copy(heads - 1).wait_recv()
    gather_mid(heads - 1, half, peer_mid)


def store_kernel(
    groups,
    counts_hbm,
    o_in,
    dq_in,
    dk_in,
    dv_in,
    cat,
    bias,
    last_back,
    o_hbm,
    dq_hbm,
    dk_hbm,
    dv_hbm,
    counts,
    p_buf,
    ds_buf,
    o_last,
    g_last,
    counts_sem,
    store_sem,
    last_sem,
):
    dest, tokens, width = o_in.shape
    orig = dq_in.shape[0]
    early, late = pl.ds(0, width - HDIM), pl.ds(width - HDIM, HDIM)
    targets = (o_hbm, dq_hbm, dk_hbm, dv_hbm)
    counts_load = pltpu.make_async_copy(counts_hbm, counts, counts_sem)
    counts_load.start()
    stores = [
        pltpu.make_async_copy(
            source.at[:, :, early], target.at[:, :, early], store_sem.at[index]
        )
        for index, (source, target) in enumerate(zip((o_in, dq_in, dk_in, dv_in), targets))
    ]
    for store in stores:
        store.start()
    counts_load.wait()
    plan = Plan(counts, groups)
    results = attend_head(plan, (dest, tokens, HDIM), cat, bias, p_buf, ds_buf)
    o_last[...] = results[0]
    for array in range(3):
        for slot in range(orig):
            g_last[array, slot] = anchor_frame(
                plan,
                slot,
                dest,
                lambda index, array=array: results[array + 1][index],
                last_back[0, array],
                last_back[1, array],
            )
    lasts = [
        pltpu.make_async_copy(source, target.at[:, :, late], last_sem.at[index])
        for index, (source, target) in enumerate(
            zip((o_last, g_last.at[0], g_last.at[1], g_last.at[2]), targets)
        )
    ]
    for store in lasts:
        store.start()
    for store in stores + lasts:
        store.wait()


def body(query_frames, key_frames, value_frames, out_cotangent, frame_counts):
    groups = lax.axis_size("group")
    orig, tokens, width = query_frames.shape
    dest = out_cotangent.shape[0]
    heads = width // HDIM
    rows = 2 * dest * tokens
    bf16 = jnp.bfloat16
    anywhere = pl.BlockSpec(memory_space=pl.ANY)
    in_vmem = pl.BlockSpec(memory_space=pltpu.VMEM)
    anchor = (orig, tokens, width)
    attending = (dest, tokens, width)
    dma = pltpu.SemaphoreType.DMA
    shapes = (attending, anchor, anchor, anchor)
    counts = frame_counts.T
    results = pl.pallas_call(
        functools.partial(kernel, groups),
        out_shape=tuple(pltpu.VMEM(shape, bf16) for shape in shapes)
        + (
            pltpu.VMEM((4, rows, HDIM), bf16),
            pltpu.VMEM((rows, rows), jnp.float32),
            pltpu.VMEM((2, 3, tokens, HDIM), bf16),
        ),
        in_specs=[anywhere] * 5,
        out_specs=(in_vmem,) * 7,
        scratch_shapes=[
            pltpu.SMEM((3, groups), jnp.int32),
            pltpu.VMEM((3,) + anchor, bf16),
            pltpu.VMEM(attending, bf16),
            pltpu.VMEM(attending, bf16),
            pltpu.VMEM((heads, 3, 2, tokens, HDIM), bf16),
            pltpu.VMEM((heads, 3, 2, tokens, HDIM), bf16),
            pltpu.VMEM((heads, 3, dest - 2, tokens, HDIM), bf16),
            pltpu.VMEM((heads, 3, dest - 2, tokens, HDIM), bf16),
            pltpu.VMEM((3, tokens, width), bf16),
            pltpu.VMEM((2, 3, tokens, width), bf16),
            pltpu.VMEM((2, heads, 3, tokens, HDIM), bf16),
            pltpu.VMEM((2, heads, 3, tokens, HDIM), bf16),
            pltpu.VMEM((heads, 3, dest, tokens, HDIM), bf16),
            pltpu.VMEM((rows, rows), bf16),
            pltpu.VMEM((rows, rows), bf16),
            pltpu.SemaphoreType.REGULAR,
            dma,
            dma((3,)),
            dma,
            dma((2,)),
            dma((2,)),
            dma,
            dma,
            dma((CHUNKS,)),
            dma((CHUNKS,)),
            dma((heads,)),
            dma((heads,)),
            dma((2,)),
            dma((2,)),
        ],
        compiler_params=pltpu.CompilerParams(
            collective_id=0, has_side_effects=True, vmem_limit_bytes=54 << 20
        ),
    )(counts, query_frames, key_frames, value_frames, out_cotangent)
    return pl.pallas_call(
        functools.partial(store_kernel, groups),
        out_shape=tuple(jax.ShapeDtypeStruct(shape, bf16) for shape in shapes),
        in_specs=[anywhere] + [in_vmem] * 7,
        out_specs=(anywhere,) * 4,
        scratch_shapes=[
            pltpu.SMEM((3, groups), jnp.int32),
            pltpu.VMEM((rows, rows), bf16),
            pltpu.VMEM((rows, rows), bf16),
            pltpu.VMEM((dest, tokens, HDIM), bf16),
            pltpu.VMEM((3, orig, tokens, HDIM), bf16),
            dma,
            dma((4,)),
            dma((4,)),
        ],
        compiler_params=pltpu.CompilerParams(vmem_limit_bytes=16 << 20),
    )(counts, *results)


def solution(mesh):
    spread = P("group", "sp", None)
    return jax.shard_map(
        body,
        mesh=mesh,
        in_specs=(spread, spread, spread, spread, P()),
        out_specs=(spread,) * 4,
        check_vma=False,
    )
```

```python
import functools
import math

import jax
import jax.numpy as jnp
from jax import lax
from jax.experimental import pallas as pl
from jax.experimental.pallas import tpu as pltpu
from jax.sharding import PartitionSpec as P

HDIM = 128
SCALING = 1.0 / math.sqrt(HDIM)
EXPONENT = SCALING * math.log2(math.e)
MESH = pl.DeviceIdType.MESH
CHUNKS = 2
AHEAD = 2
PAIRS = 7
EDGE_UNROLL = 5
GATHER_FROM = 8
ROW_BLOCKS = 4


def pick(cond, yes, no):
    return lax.select_n(cond, no, yes)


def dot(left, right, dims):
    return lax.dot_general(left, right, (dims, ((), ())), preferred_element_type=jnp.float32)


def attend(queries, keys, values, upstream, mask):
    logits = dot(queries, keys, ((1,), (1,))) * EXPONENT + mask
    powers = jnp.exp2(logits - jnp.max(logits, axis=1, keepdims=True))
    softmax = powers * (1.0 / jnp.sum(powers, axis=1, keepdims=True))
    prob_grad = dot(upstream, values, ((1,), (1,)))
    correction = jnp.sum(softmax * prob_grad, axis=1, keepdims=True)
    logit_grad = softmax * (prob_grad - correction)
    return softmax.astype(jnp.bfloat16), logit_grad.astype(jnp.bfloat16)


def attend_head(plan, shape, cat, bias, p_buf, ds_buf):
    tokens = shape[1]
    rows = cat.shape[1]
    half = rows // 2
    edge = half - tokens
    size = rows // ROW_BLOCKS
    for block in range(ROW_BLOCKS):
        span = pl.ds(block * size, size)
        p_buf[span], ds_buf[span] = attend(cat[0, span], cat[1], cat[2], cat[3, span], bias[span])
    probs = jnp.concatenate(
        [
            pick(plan.swap_low, p_buf[half : half + tokens], p_buf[:tokens]),
            p_buf[tokens:edge],
            pick(plan.swap_high, p_buf[half + edge :], p_buf[edge:half]),
        ],
        axis=0,
    )
    attended = dot(probs, cat[2], ((1,), (0,)))
    query_grad = dot(ds_buf[:half], cat[1], ((1,), (0,))) * SCALING
    key_grad = dot(ds_buf[:, :half], cat[0], ((0,), (0,))) * SCALING
    value_grad = dot(p_buf[:, :half], cat[3], ((0,), (0,)))
    results = (attended, query_grad, key_grad, value_grad)
    return [result.astype(jnp.bfloat16).reshape(shape) for result in results]


class Plan:
    def __init__(self, counts, groups):
        g = lax.axis_index("group")
        core = g % 2
        upper = (g + 1) % groups
        lower = (g + groups - 1) % groups
        self.take_low = counts[0, g]
        self.take_high = counts[2, g]
        self.give_low = counts[2, lower]
        self.give_high = counts[0, upper]
        self.shift = self.give_low - self.take_low
        self.last_slot = self.give_low + counts[1, g]
        self.from_low = self.take_low == 1
        self.from_high = self.take_high == 1
        self.swap_low = jnp.logical_and(core == 0, self.from_low)
        self.swap_high = jnp.logical_and(core == 1, self.from_high)


def anchor_frame(plan, slot, dest, grad, low_back, high_back):
    zero = jnp.zeros_like(low_back)

    def source(index):
        return grad(index) if 0 <= index < dest else zero

    frame = pick(plan.shift == 1, source(slot - 1), source(slot))
    frame = pick(plan.shift == -1, source(slot + 1), frame)
    inside = jnp.logical_and(slot >= plan.give_low, slot < plan.last_slot)
    frame = pick(inside, frame, zero)
    if slot == 0:
        frame = pick(plan.give_low == 1, low_back, frame)
    if slot >= dest - 2:
        top = jnp.logical_and(plan.last_slot == slot, plan.give_high == 1)
        frame = pick(top, high_back, frame)
    return frame


def kernel(
    groups,
    counts_hbm,
    q_hbm,
    k_hbm,
    v_hbm,
    do_hbm,
    o_out,
    dq_out,
    dk_out,
    dv_out,
    cat,
    bias,
    last_back,
    counts,
    raw,
    own_do,
    peer_do,
    own_edge,
    peer_edge,
    own_mid,
    peer_mid,
    move_src,
    move_dst,
    back_src,
    back_dst,
    grads,
    p_buf,
    ds_buf,
    ready,
    counts_sem,
    raw_sem,
    up_sem,
    move_send,
    move_recv,
    do_send,
    do_recv,
    edge_send,
    edge_recv,
    mid_send,
    mid_recv,
    back_send,
    back_recv,
):
    heads = own_mid.shape[0]
    dest, tokens, _ = own_do.shape
    orig = raw.shape[1]
    inner = dest - 2
    half = dest * tokens
    rows = 2 * half
    edge_slots = (0, dest - 1)
    group_heads = heads // CHUNKS

    g = lax.axis_index("group")
    s = lax.axis_index("sp")
    core = g % 2
    upper = (g + 1) % groups
    lower = (g + groups - 1) % groups
    flip = 1 - 2 * s
    to_peer = {"group": g, "sp": 1 - s}
    to_upper = {"group": upper, "sp": s + core * flip}
    to_lower = {"group": lower, "sp": s + (1 - core) * flip}

    def cols(h):
        return pl.ds(pl.multiple_of(h * HDIM, HDIM), HDIM)

    def raw_load(array):
        source = (q_hbm, k_hbm, v_hbm)[array]
        return pltpu.make_async_copy(source, raw.at[array], raw_sem.at[array])

    up_load = pltpu.make_async_copy(do_hbm, own_do, up_sem)

    def remote(src, dst, send, recv, device):
        return pltpu.make_async_remote_copy(
            src_ref=src,
            dst_ref=dst,
            send_sem=send,
            recv_sem=recv,
            device_id=device,
            device_id_type=MESH,
        )

    def move(way):
        source = move_src if way == 0 else raw.at[:, 0]
        return remote(
            source,
            move_dst.at[way],
            move_send.at[way],
            move_recv.at[way],
            to_upper if way == 0 else to_lower,
        )

    do_copy = remote(do_hbm, peer_do, do_send, do_recv, to_peer)

    def edge_copy(chunk):
        span = pl.ds(chunk * group_heads, group_heads)
        return remote(
            own_edge.at[span],
            peer_edge.at[span],
            edge_send.at[chunk],
            edge_recv.at[chunk],
            to_peer,
        )

    def mid_copy(h):
        return remote(own_mid.at[h], peer_mid.at[h], mid_send.at[h], mid_recv.at[h], to_peer)

    def pair_copy(pair):
        span, h = pl.ds(2 * pair, 2), 2 * pair
        return remote(own_mid.at[span], peer_mid.at[span], mid_send.at[h], mid_recv.at[h], to_peer)

    def back(way):
        return remote(
            back_src.at[way],
            back_dst.at[way],
            back_send.at[way],
            back_recv.at[way],
            to_upper if way == 0 else to_lower,
        )

    def each(low, high, action):
        def step(h, carry):
            action(h)
            return carry

        lax.fori_loop(low, high, step, 0)

    barrier = pltpu.get_barrier_semaphore()
    pl.semaphore_signal(barrier, inc=1, device_id=to_peer, device_id_type=MESH)

    @pl.when(core == 1)
    def _():
        for device in (to_upper, to_lower):
            pl.semaphore_signal(barrier, inc=1, device_id=device, device_id_type=MESH)

    counts_load = pltpu.make_async_copy(counts_hbm, counts, counts_sem)
    counts_load.start()
    for array in range(3):
        raw_load(array).start()
    up_load.start()

    @pl.when(core == 1)
    def _():
        pl.semaphore_wait(barrier, 1)

    @pl.when(core == 0)
    def _():
        pl.semaphore_wait(barrier, 3)

    do_copy.start()

    @pl.when(core == 0)
    def _():
        for device in (to_upper, to_lower):
            pl.semaphore_signal(ready, inc=1, device_id=device, device_id_type=MESH)

    counts_load.wait()
    plan = Plan(counts, groups)
    for array in range(3):
        raw_load(array).wait()

    def stage_move(h):
        for array in range(3):
            frame = raw[array, orig - 1, :, cols(h)]
            for slot in range(inner, orig - 1):
                frame = pick(plan.last_slot == slot, raw[array, slot, :, cols(h)], frame)
            move_src[array, :, cols(h)] = frame

    each(0, heads, stage_move)

    @pl.when(core == 1)
    def _():
        pl.semaphore_wait(ready, 2)

    move(1).start()
    move(0).start()

    def native_frame(h, array, slot):
        here = raw[array, slot, :, cols(h)]
        frame = pick(plan.shift == 1, raw[array, slot + 1, :, cols(h)], here)
        if slot > 0:
            frame = pick(plan.shift == -1, raw[array, slot - 1, :, cols(h)], frame)
        return frame

    def stage_mid(h):
        for array in range(3):
            for slot in range(inner):
                own_mid[h, array, slot] = native_frame(h, array, slot + 1)

    each(0, heads, stage_mid)

    def labels(dim):
        slot = (lax.broadcasted_iota(jnp.int32, (rows, rows), dim) // tokens) % dest
        low = jnp.where(slot == 0, plan.take_low, 0)
        high = jnp.where(slot == dest - 1, plan.take_high, 0)
        return high - low

    bias[...] = jnp.where(labels(0) == labels(1), 0.0, -jnp.inf)

    move(0).wait_recv()
    move(1).wait_recv()

    def stage_edge(h):
        for array in range(3):
            for way, (slot, moved) in enumerate(
                ((0, plan.from_low), (dest - 1, plan.from_high))
            ):
                frame = native_frame(h, array, slot)
                own_edge[h, array, way] = pick(moved, move_dst[way, array, :, cols(h)], frame)

    for chunk in range(CHUNKS):
        each(chunk * group_heads, (chunk + 1) * group_heads, stage_edge)
        edge_copy(chunk).start()

    def edge_up(h, way):
        slot, swap = ((0, plan.swap_low), (dest - 1, plan.swap_high))[way]
        mine, other = own_do[slot, :, cols(h)], peer_do[slot, :, cols(h)]
        return pick(swap, other, mine), pick(swap, mine, other)

    edge_row = lax.broadcasted_iota(jnp.int32, (4 * tokens, 4 * tokens), 0) // tokens % 2
    edge_col = lax.broadcasted_iota(jnp.int32, (4 * tokens, 4 * tokens), 1) // tokens % 2
    edge_mask = jnp.where(edge_row == edge_col, 0.0, -jnp.inf)

    def edge_compute(h):
        def joined(array):
            both = [ref[h, array].reshape(2 * tokens, HDIM) for ref in (own_edge, peer_edge)]
            return jnp.concatenate(both, axis=0)

        queries, keys, values = joined(0), joined(1), joined(2)
        (low, far_low), (high, far_high) = edge_up(h, 0), edge_up(h, 1)
        upstream = jnp.concatenate([low, high, far_low, far_high], axis=0)
        probs, logit_grad = attend(queries, keys, values, upstream, edge_mask)
        mine = 2 * tokens
        query_grad = dot(logit_grad[:mine], keys, ((1,), (0,))) * SCALING
        key_grad = dot(logit_grad[:, :mine], queries, ((0,), (0,))) * SCALING
        value_grad = dot(probs[:, :mine], upstream, ((0,), (0,)))
        for array, grad in enumerate((query_grad, key_grad, value_grad)):
            grad = grad.astype(jnp.bfloat16)
            back_src[1, h, array] = grad[:tokens]
            back_src[0, h, array] = grad[tokens:]

    def gather_mid(h, base, mids):
        for array in range(3):
            cat[array, pl.ds(base + tokens, inner * tokens)] = mids[h, array].reshape(
                inner * tokens, HDIM
            )

    def gather(h):
        edge = half - tokens
        gather_mid(h, 0, own_mid)
        for array in range(3):
            for base, edges in ((0, own_edge), (half, peer_edge)):
                cat[array, pl.ds(base, tokens)] = edges[h, array, 0]
                cat[array, pl.ds(base + edge, tokens)] = edges[h, array, 1]
        for slot in range(1, dest - 1):
            cat[3, pl.ds(slot * tokens, tokens)] = own_do[slot, :, cols(h)]
            cat[3, pl.ds(half + slot * tokens, tokens)] = peer_do[slot, :, cols(h)]
        for way, slot in enumerate(edge_slots):
            mine, other = edge_up(h, way)
            cat[3, pl.ds(slot * tokens, tokens)] = mine
            cat[3, pl.ds(half + slot * tokens, tokens)] = other

    def compute(h):
        results = attend_head(plan, (dest, tokens, HDIM), cat, bias, p_buf, ds_buf)
        o_out[:, :, cols(h)] = results[0]
        for array in range(3):
            grads[h, array] = results[array + 1]

    def assemble(h):
        for array in range(3):
            for slot in range(orig):
                (dq_out, dk_out, dv_out)[array][slot, :, cols(h)] = anchor_frame(
                    plan,
                    slot,
                    dest,
                    lambda index, array=array: grads[h, array, index],
                    back_dst[0, h, array],
                    back_dst[1, h, array],
                )

    up_load.wait()
    do_copy.wait_send()
    each(0, AHEAD, lambda pair: pair_copy(pair).start())
    do_copy.wait_recv()
    for chunk in range(CHUNKS):
        edge_copy(chunk).wait_recv()

        def edge_step(step, carry):
            for part in range(EDGE_UNROLL):
                edge_compute(step * EDGE_UNROLL + part)
            return carry

        count = group_heads // EDGE_UNROLL
        lax.fori_loop(chunk * count, (chunk + 1) * count, edge_step, 0)
    back(0).start()
    back(1).start()

    def main_step(h):
        gather(h)

        @pl.when(jnp.logical_and(h < 2 * PAIRS, h % 2 == 0))
        def _():
            pair = h // 2

            @pl.when(pair + AHEAD < PAIRS)
            def _():
                pair_copy(pair + AHEAD).start()

            pair_copy(pair).wait_recv()

        @pl.when(h == 2 * PAIRS - 6)
        def _():
            each(2 * PAIRS, heads, lambda late: mid_copy(late).start())

        @pl.when(h >= 2 * PAIRS)
        def _():
            mid_copy(h).wait_recv()

        gather_mid(h, half, peer_mid)
        compute(h)

        @pl.when(h == GATHER_FROM)
        def _():
            back(0).wait_recv()
            back(1).wait_recv()
            each(0, GATHER_FROM, assemble)

        @pl.when(h >= GATHER_FROM)
        def _():
            assemble(h)

    each(0, heads - 1, main_step)
    last_back[...] = back_dst[:, heads - 1]
    gather(heads - 1)
    for chunk in range(CHUNKS):
        edge_copy(chunk).wait_send()
    for way in range(2):
        move(way).wait_send()
        back(way).wait_send()
    each(0, PAIRS, lambda pair: pair_copy(pair).wait_send())
    each(2 * PAIRS, heads, lambda h: mid_copy(h).wait_send())
    mid_copy(heads - 1).wait_recv()
    gather_mid(heads - 1, half, peer_mid)


def store_kernel(
    groups,
    counts_hbm,
    o_in,
    dq_in,
    dk_in,
    dv_in,
    cat,
    bias,
    last_back,
    o_hbm,
    dq_hbm,
    dk_hbm,
    dv_hbm,
    counts,
    p_buf,
    ds_buf,
    o_last,
    g_last,
    counts_sem,
    store_sem,
    last_sem,
):
    dest, tokens, width = o_in.shape
    orig = dq_in.shape[0]
    early, late = pl.ds(0, width - HDIM), pl.ds(width - HDIM, HDIM)
    targets = (o_hbm, dq_hbm, dk_hbm, dv_hbm)
    counts_load = pltpu.make_async_copy(counts_hbm, counts, counts_sem)
    counts_load.start()
    stores = [
        pltpu.make_async_copy(
            source.at[:, :, early], target.at[:, :, early], store_sem.at[index]
        )
        for index, (source, target) in enumerate(zip((o_in, dq_in, dk_in, dv_in), targets))
    ]
    for store in stores:
        store.start()
    counts_load.wait()
    plan = Plan(counts, groups)
    results = attend_head(plan, (dest, tokens, HDIM), cat, bias, p_buf, ds_buf)
    o_last[...] = results[0]
    for array in range(3):
        for slot in range(orig):
            g_last[array, slot] = anchor_frame(
                plan,
                slot,
                dest,
                lambda index, array=array: results[array + 1][index],
                last_back[0, array],
                last_back[1, array],
            )
    lasts = [
        pltpu.make_async_copy(source, target.at[:, :, late], last_sem.at[index])
        for index, (source, target) in enumerate(
            zip((o_last, g_last.at[0], g_last.at[1], g_last.at[2]), targets)
        )
    ]
    for store in lasts:
        store.start()
    for store in stores + lasts:
        store.wait()


def body(query_frames, key_frames, value_frames, out_cotangent, frame_counts):
    groups = lax.axis_size("group")
    orig, tokens, width = query_frames.shape
    dest = out_cotangent.shape[0]
    heads = width // HDIM
    rows = 2 * dest * tokens
    bf16 = jnp.bfloat16
    anywhere = pl.BlockSpec(memory_space=pl.ANY)
    in_vmem = pl.BlockSpec(memory_space=pltpu.VMEM)
    anchor = (orig, tokens, width)
    attending = (dest, tokens, width)
    dma = pltpu.SemaphoreType.DMA
    shapes = (attending, anchor, anchor, anchor)
    counts = frame_counts.T
    results = pl.pallas_call(
        functools.partial(kernel, groups),
        out_shape=tuple(pltpu.VMEM(shape, bf16) for shape in shapes)
        + (
            pltpu.VMEM((4, rows, HDIM), bf16),
            pltpu.VMEM((rows, rows), jnp.float32),
            pltpu.VMEM((2, 3, tokens, HDIM), bf16),
        ),
        in_specs=[anywhere] * 5,
        out_specs=(in_vmem,) * 7,
        scratch_shapes=[
            pltpu.SMEM((3, groups), jnp.int32),
            pltpu.VMEM((3,) + anchor, bf16),
            pltpu.VMEM(attending, bf16),
            pltpu.VMEM(attending, bf16),
            pltpu.VMEM((heads, 3, 2, tokens, HDIM), bf16),
            pltpu.VMEM((heads, 3, 2, tokens, HDIM), bf16),
            pltpu.VMEM((heads, 3, dest - 2, tokens, HDIM), bf16),
            pltpu.VMEM((heads, 3, dest - 2, tokens, HDIM), bf16),
            pltpu.VMEM((3, tokens, width), bf16),
            pltpu.VMEM((2, 3, tokens, width), bf16),
            pltpu.VMEM((2, heads, 3, tokens, HDIM), bf16),
            pltpu.VMEM((2, heads, 3, tokens, HDIM), bf16),
            pltpu.VMEM((heads, 3, dest, tokens, HDIM), bf16),
            pltpu.VMEM((rows, rows), bf16),
            pltpu.VMEM((rows, rows), bf16),
            pltpu.SemaphoreType.REGULAR,
            dma,
            dma((3,)),
            dma,
            dma((2,)),
            dma((2,)),
            dma,
            dma,
            dma((CHUNKS,)),
            dma((CHUNKS,)),
            dma((heads,)),
            dma((heads,)),
            dma((2,)),
            dma((2,)),
        ],
        compiler_params=pltpu.CompilerParams(
            collective_id=0, has_side_effects=True, vmem_limit_bytes=54 << 20
        ),
    )(counts, query_frames, key_frames, value_frames, out_cotangent)
    return pl.pallas_call(
        functools.partial(store_kernel, groups),
        out_shape=tuple(jax.ShapeDtypeStruct(shape, bf16) for shape in shapes),
        in_specs=[anywhere] + [in_vmem] * 7,
        out_specs=(anywhere,) * 4,
        scratch_shapes=[
            pltpu.SMEM((3, groups), jnp.int32),
            pltpu.VMEM((rows, rows), bf16),
            pltpu.VMEM((rows, rows), bf16),
            pltpu.VMEM((dest, tokens, HDIM), bf16),
            pltpu.VMEM((3, orig, tokens, HDIM), bf16),
            dma,
            dma((4,)),
            dma((4,)),
        ],
        compiler_params=pltpu.CompilerParams(vmem_limit_bytes=16 << 20),
    )(counts, *results)


def solution(mesh):
    spread = P("group", "sp", None)
    return jax.shard_map(
        body,
        mesh=mesh,
        in_specs=(spread, spread, spread, spread, P()),
        out_specs=(spread,) * 4,
        check_vma=False,
    )
```
